256 devices in a mesh: frame: 8 (over z_hi, core), tile: 32 (over z_lo, y, x).
Axes of the slice: x: 4, y: 4, z: 8 (z_hi: 4, z_lo: 2; z = z_hi * 2 + z_lo), core: 2. Of those that a mesh axis runs over, the one named last changes fastest.
Arguments:
- queries: bfloat16 [32768, 4096], P(('frame', 'tile')), may hold values from -100 to 100
- keys: bfloat16 [32768, 4096], P(('frame', 'tile')), may hold values from -6 to 6
- values: bfloat16 [32768, 4096], P(('frame', 'tile')), may hold values from -6 to 6
- out_grad: bfloat16 [32768, 4096], P(('frame', 'tile')), may hold values from -6 to 6
- key_lists: int32 [256, 6], P('frame'), may hold values from 0 to 95, as said below
- key_counts: int32 [256], P('frame'), may hold values from 2 to 6
Outputs:
- query_grad: bfloat16 [32768, 4096], P(('frame', 'tile'))
- key_grad: bfloat16 [32768, 4096], P(('frame', 'tile'))
- value_grad: bfloat16 [32768, 4096], P(('frame', 'tile'))
The draws below stay inside these ranges and needn't reach their ends.
Inputs may be any that keep to these rules, and one draw needn't show every extreme that they name: `key_lists`: each row holds distinct window positions; its first entry is the query's own block, and no entry names a block outside the clip. All entries of the rows of one frame group together name at most 16 distinct blocks of the previous group and at most 16 of the next.
All inputs are finite; a program needn't handle non-finite values.
Results may differ from the reference program's by a relative error of at most 0.0052.
Values may be sent and summed in bfloat16 or wider, within the bound.
A program may use at most 128 MiB of HBM per device.

```python
import jax
import jax.numpy as jnp
from jax import lax

HEADS = 32
HEAD_DIM = 128
BLOCK = 128
MAXK = 6
TOKENS = 32768
FRAME_BLOCKS = 32
QBLOCKS = 256
NEAR = 16


def shared_field(key):
    return jax.random.truncated_normal(key, -6.0, 6.0, (TOKENS, HEADS * HEAD_DIM), jnp.float32)


def draw_keys(key, part):
    return shared_field(key).astype(jnp.bfloat16)


def draw_queries(key, part):
    key = jax.random.fold_in(key, 2)
    fresh = jax.random.truncated_normal(key, -6.0, 6.0, (TOKENS, HEADS * HEAD_DIM), jnp.float32)
    return fresh.astype(jnp.bfloat16)


def draw_key_lists(key, part):
    key = jax.random.fold_in(key, 3)
    pick_key, noise_key, order_key = jax.random.split(key, 3)
    span = 3 * FRAME_BLOCKS
    frames = QBLOCKS // FRAME_BLOCKS
    block_ids = jnp.arange(FRAME_BLOCKS, dtype=jnp.int32)
    frame_ids = jnp.arange(frames, dtype=jnp.int32)[:, None, None]
    side_ids = jnp.arange(2, dtype=jnp.int32)[None, :, None]
    rank = jax.random.randint(pick_key, (frames, 2, FRAME_BLOCKS), 0, 1000, jnp.int32)
    edges = (frame_ids == 0) & (side_ids == 1) & (block_ids == FRAME_BLOCKS - 1) | (frame_ids == frames - 1) & (side_ids == 0) & (block_ids == 0)
    rank = (rank + 1000 * edges.astype(jnp.int32)) * FRAME_BLOCKS + block_ids
    _, chosen = lax.top_k(rank, NEAR)
    chosen = chosen.astype(jnp.int32)
    member = jnp.any(chosen[:, :, :, None] == block_ids[None, None, None, :], axis=2)
    rows = jnp.arange(QBLOCKS, dtype=jnp.int32)[:, None]
    cols = jnp.arange(span, dtype=jnp.int32)[None, :]
    frame = rows // FRAME_BLOCKS
    local = rows % FRAME_BLOCKS
    prev_ok = member[frame[:, 0], 0]
    next_ok = member[frame[:, 0], 1]
    eligible = jnp.concatenate([prev_ok, jnp.ones((QBLOCKS, FRAME_BLOCKS), bool), next_ok], 1)
    side = (local >= NEAR).astype(jnp.int32)
    target_block = chosen[frame[:, 0], side[:, 0], local[:, 0] % NEAR][:, None]
    forced = cols == target_block + 2 * FRAME_BLOCKS * side
    noise = jax.random.randint(noise_key, (QBLOCKS, span), 0, 1000, jnp.int32)
    own = (cols >= FRAME_BLOCKS) & (cols < 2 * FRAME_BLOCKS)
    diag = cols == FRAME_BLOCKS + local
    outside = (frame == 0) & (cols < FRAME_BLOCKS) | (frame == frames - 1) & (cols >= 2 * FRAME_BLOCKS)
    score = noise + 100 * own.astype(jnp.int32) + 100000 * diag.astype(jnp.int32) + 50000 * (forced & ~outside).astype(jnp.int32) - 20000 * outside.astype(jnp.int32) - 20000 * (~eligible).astype(jnp.int32)
    score = score * 1024 + cols
    _, picked = lax.top_k(score, MAXK)
    slot = jnp.arange(MAXK, dtype=jnp.int32)[None, :]
    shuffle = jax.random.randint(order_key, (QBLOCKS, MAXK), 0, 1000, jnp.int32) * MAXK + slot
    shuffle = jnp.where(slot == 0, 1 << 30, shuffle)
    _, order = lax.top_k(shuffle, MAXK)
    return jnp.take_along_axis(picked.astype(jnp.int32), order.astype(jnp.int32), axis=1).astype(jnp.int32)


def draw_key_counts(key, part):
    key = jax.random.fold_in(key, 4)
    first, second = jax.random.split(key)
    counts = jax.random.randint(first, (QBLOCKS,), 2, MAXK + 1, jnp.int32)
    place = jax.random.randint(second, (), 0, QBLOCKS, jnp.int32)
    return jnp.where(jnp.arange(QBLOCKS, dtype=jnp.int32) == place, MAXK, counts).astype(jnp.int32)


def shard_levels(rng, extent, cuts, smallest, largest):
    loudness = 1.0
    for dim, shards_of in cuts:
        heights = jax.random.uniform(jax.random.fold_in(jax.random.fold_in(rng, 6), dim), (shards_of,), jnp.float32, smallest / len(cuts), largest / len(cuts))
        loudness = loudness * jnp.repeat(jnp.exp(heights), extent[dim] // shards_of).reshape((-1,) + (1,) * (len(extent) - 1 - dim))
    return loudness


def gaussian(rng, shape, scale, limit, cuts=(), held_as=jnp.bfloat16):
    values = jax.random.normal(rng, shape, jnp.float32) * scale
    if len(cuts) > 0:
        values = shard_levels(rng, shape, cuts, -0.22, 0.18) * values
    return jnp.clip(values, min=-limit, max=limit).astype(held_as)


def setup_inputs(seed: int = 0) -> dict:
    key_of = jax.random.split(jax.random.key(seed), 7)
    return {
        "queries": draw_queries(jax.random.fold_in(key_of[6], 71), 0),
        "keys": draw_keys(jax.random.fold_in(key_of[6], 71), 0),
        "values": gaussian(key_of[2], (TOKENS, HEADS * HEAD_DIM), 1.0, 6.0, ((0, 256),)),
        "out_grad": gaussian(key_of[3], (TOKENS, HEADS * HEAD_DIM), 1.0, 6.0, ((0, 256),)),
        "key_lists": draw_key_lists(jax.random.fold_in(key_of[6], 71), 0),
        "key_counts": draw_key_counts(jax.random.fold_in(key_of[6], 71), 0),
    }


def low(x):
    return lax.optimization_barrier(x.astype(jnp.bfloat16)).astype(jnp.float32)


def attend_back(q_blocks, g_blocks, k_all, v_all, gather_idx, scatter_idx, targets, valid, scale):
    qf = q_blocks.astype(jnp.float32)
    gf = g_blocks.astype(jnp.float32)
    slots = gather_idx.shape[1]
    nblk, rows, heads, width = qf.shape

    def scores(s):
        kb = k_all[gather_idx[:, s]].astype(jnp.float32)
        return jnp.einsum('nahd,nbhd->nhab', qf, kb) * scale, kb

    top = jnp.full((nblk, heads, rows), -1e30, jnp.float32)
    for s in range(slots):
        sc, _ = scores(s)
        top = jnp.where(valid[:, s][:, None, None], jnp.maximum(top, sc.max(-1)), top)
    total = jnp.zeros((nblk, heads, rows), jnp.float32)
    for s in range(slots):
        sc, _ = scores(s)
        total = total + jnp.where(valid[:, s][:, None, None], jnp.exp(sc - top[..., None]).sum(-1), 0.0)
    lse = top + jnp.log(total)

    def probs(s):
        sc, kb = scores(s)
        vb = v_all[gather_idx[:, s]].astype(jnp.float32)
        prob = jnp.where(valid[:, s][:, None, None, None], jnp.exp(sc - lse[..., None]), 0.0)
        return prob, kb, vb

    attn_out = jnp.zeros(qf.shape, jnp.float32)
    for s in range(slots):
        prob, kb, vb = probs(s)
        attn_out = attn_out + jnp.einsum('nhab,nbhd->nahd', low(prob), vb)
    delta = jnp.sum(gf * attn_out, axis=3).transpose(0, 2, 1)
    dq = jnp.zeros(qf.shape, jnp.float32)
    dk = jnp.zeros((targets,) + k_all.shape[1:], jnp.float32)
    dv = jnp.zeros((targets,) + k_all.shape[1:], jnp.float32)
    for s in range(slots):
        prob, kb, vb = probs(s)
        dprob = jnp.einsum('nahd,nbhd->nhab', gf, vb)
        dscore = low(prob * (dprob - delta[..., None]))
        plow = low(prob)
        dq = dq + jnp.einsum('nhab,nbhd->nahd', dscore, kb)
        dk = dk.at[scatter_idx[:, s]].add(jnp.einsum('nhab,nahd->nbhd', dscore, qf))
        dv = dv.at[scatter_idx[:, s]].add(jnp.einsum('nhab,nahd->nbhd', plow, gf))
    return dq * scale, dk * scale, dv


def reference(queries, keys, values, out_grad, key_lists, key_counts):
    scale = HEAD_DIM ** -0.5
    frames = QBLOCKS // FRAME_BLOCKS
    span = 3 * FRAME_BLOCKS

    def heads(x):
        return x.reshape(QBLOCKS, BLOCK, HEADS, HEAD_DIM).transpose(2, 0, 1, 3)[:, :, :, None, :]

    frame_of = (jnp.arange(QBLOCKS) // FRAME_BLOCKS).astype(jnp.int32)
    gather_idx = jnp.clip((frame_of - 1)[:, None] * FRAME_BLOCKS + key_lists, 0, QBLOCKS - 1).astype(jnp.int32)
    scatter_idx = (frame_of[:, None] * span + key_lists).astype(jnp.int32)
    valid = jnp.arange(MAXK)[None, :] < key_counts[:, None]

    def settle(window):
        window = window.reshape(frames, span, BLOCK, 1, HEAD_DIM)
        own = window[:, FRAME_BLOCKS:2 * FRAME_BLOCKS]
        blank = jnp.zeros_like(own[:1])
        later = jnp.concatenate([window[1:, :FRAME_BLOCKS], blank], 0)
        earlier = jnp.concatenate([blank, window[:-1, 2 * FRAME_BLOCKS:]], 0)
        return (own + low(later) + low(earlier)).reshape(QBLOCKS, BLOCK, 1, HEAD_DIM).astype(jnp.bfloat16)

    def one_head(parts):
        q_head, k_head, v_head, g_head = parts
        dq, dk, dv = attend_back(q_head, g_head, k_head, v_head, gather_idx, scatter_idx, frames * span, valid, scale)
        return dq.astype(jnp.bfloat16), settle(dk), settle(dv)

    dq, dk, dv = lax.map(one_head, (heads(queries), heads(keys), heads(values), heads(out_grad)))

    def back(x):
        return x[:, :, :, 0, :].transpose(1, 2, 0, 3).reshape(TOKENS, HEADS * HEAD_DIM)

    return back(dq), back(dk), back(dv)
```

```python
import functools

import jax
import jax.numpy as jnp
from jax import lax
from jax.experimental import pallas as pl
from jax.experimental.pallas import tpu as pltpu
from jax.sharding import PartitionSpec as P

D = 128
NEAR = 16
MESH = pl.DeviceIdType.MESH
ANY = pl.BlockSpec(memory_space=pl.ANY)
SMEM = pl.BlockSpec(memory_space=pltpu.SMEM)
VMEM = pl.BlockSpec(memory_space=pltpu.VMEM)
LOG2E = 1.4426950408889634


def peer_of(i, me, tiles):
    half = tiles // 2
    z, y, x = me // half, (me % half) // 4, me % 4
    z = (z + i) % 2
    x = (x + i // 2) % 4
    y = (y + i // 8) % (half // 4)
    return z * half + y * 4 + x


def greet(tiles, me, before, after):
    barrier = pltpu.get_barrier_semaphore()

    def hello(i, carry):
        pl.semaphore_signal(barrier, inc=1, device_id={"tile": peer_of(i, me, tiles)}, device_id_type=MESH)
        return carry

    lax.fori_loop(1, tiles, hello, 0)
    for frame in (before, after):
        pl.semaphore_signal(barrier, inc=1, device_id={"frame": frame}, device_id_type=MESH)
    pl.semaphore_wait(barrier, tiles + 1)


def wait_bytes(ref, sem):
    pltpu.make_async_copy(ref, ref, sem).wait()


def gather_kernel(tiles, frames, pick_ref, q_ref, k_ref, v_ref, g_ref, q_out, g_out, kv_out,
                  own, packed, send_sem, recv_sem, local_sem, near_send, near_recv):
    me, frame = lax.axis_index("tile"), lax.axis_index("frame")
    before, after = (frame + frames - 1) % frames, (frame + 1) % frames
    greet(tiles, me, before, after)

    places = (
        (k_ref, lambda t: own.at[t, :, pl.ds(0, D)]),
        (v_ref, lambda t: own.at[t, :, pl.ds(D, D)]),
        (q_ref, lambda t: q_out.at[t]),
        (g_ref, lambda t: g_out.at[t]),
    )
    for a, (src, place) in enumerate(places):
        def send(i, carry, a=a, src=src, place=place):
            to = peer_of(i, me, tiles)
            pltpu.make_async_remote_copy(
                src_ref=src.at[:, pl.ds(pl.multiple_of(to * D, D), D)], dst_ref=place(me),
                send_sem=send_sem.at[a], recv_sem=recv_sem.at[a],
                device_id={"tile": to}, device_id_type=MESH,
            ).start()
            return carry

        lax.fori_loop(1, tiles, send, 0)
        pltpu.make_async_copy(
            src.at[:, pl.ds(pl.multiple_of(me * D, D), D)], place(me), local_sem.at[a]
        ).start()

    for a in range(2):
        wait_bytes(own.at[pl.ds(0, tiles - 1), :, pl.ds(0, D)], recv_sem.at[a])
        pltpu.make_async_copy(
            places[a][0].at[:, pl.ds(pl.multiple_of(me * D, D), D)], places[a][1](me), local_sem.at[a]
        ).wait()

    keep = pltpu.make_async_copy(own, kv_out.at[pl.ds(0, tiles)], local_sem.at[4])
    keep.start()
    near = []
    for side, frame_to in ((0, before), (1, after)):
        def pack(n, carry, side=side):
            packed[side, n] = own[pick_ref[side * NEAR + n]]
            return carry

        lax.fori_loop(0, NEAR, pack, 0)
        copy = pltpu.make_async_remote_copy(
            src_ref=packed.at[side], dst_ref=kv_out.at[pl.ds(tiles + (1 - side) * NEAR, NEAR)],
            send_sem=near_send.at[side], recv_sem=near_recv.at[side],
            device_id={"frame": frame_to}, device_id_type=MESH,
        )
        copy.start()
        near.append(copy)

    for a in range(2, 4):
        wait_bytes(q_out.at[pl.ds(0, tiles - 1)], recv_sem.at[a])
        pltpu.make_async_copy(
            places[a][0].at[:, pl.ds(pl.multiple_of(me * D, D), D)], places[a][1](me), local_sem.at[a]
        ).wait()
    for a in range(4):
        wait_bytes(q_out.at[pl.ds(0, tiles - 1)], send_sem.at[a])
    keep.wait()
    for copy in near:
        copy.wait()


def gather(tiles, frames, pick, q, k, v, g):
    bf16 = jnp.bfloat16
    return pl.pallas_call(
        functools.partial(gather_kernel, tiles, frames),
        out_shape=(
            jax.ShapeDtypeStruct((tiles, D, D), bf16),
            jax.ShapeDtypeStruct((tiles, D, D), bf16),
            jax.ShapeDtypeStruct((tiles + 2 * NEAR, D, 2 * D), bf16),
        ),
        in_specs=[SMEM, ANY, ANY, ANY, ANY],
        out_specs=(ANY, ANY, ANY),
        scratch_shapes=[
            pltpu.VMEM((tiles, D, 2 * D), bf16),
            pltpu.VMEM((2, NEAR, D, 2 * D), bf16),
            pltpu.SemaphoreType.DMA((4,)),
            pltpu.SemaphoreType.DMA((4,)),
            pltpu.SemaphoreType.DMA((5,)),
            pltpu.SemaphoreType.DMA((2,)),
            pltpu.SemaphoreType.DMA((2,)),
        ],
        compiler_params=pltpu.CompilerParams(
            collective_id=0, has_side_effects=True, vmem_limit_bytes=32 * 2**20
        ),
        name="gather",
    )(pick, q, k, v, g)


def attend_kernel(lists_ref, counts_ref, q_ref, g_ref, kv_ref, dq_ref, own_ref, near_ref, kt, acc):
    nblk = q_ref.shape[0]
    slots = lists_ref.shape[1]
    nkey = kv_ref.shape[0]
    scale = D ** (-0.5)

    def prepare(j, carry):
        kt[j] = kv_ref[j, :, 0:D].T
        acc[j] = jnp.zeros_like(acc[j])
        return carry

    lax.fori_loop(0, nkey, prepare, 0)

    def block(r, carry):
        q, g = q_ref[r], g_ref[r]
        zero = jnp.zeros_like(q)
        both = jnp.concatenate([jnp.concatenate([q, zero], 1), jnp.concatenate([zero, g], 1)], 0)
        count = counts_ref[r]
        idx = [lists_ref[r, s] for s in range(slots)]
        score, dprob, top = [], [], None
        for s in range(slots):
            out = lax.dot_general(
                kv_ref[idx[s]], both, (((1,), (1,)), ((), ())), preferred_element_type=jnp.float32
            )
            sc = out[:, :D] * (scale * LOG2E)
            if s >= 2:
                sc = jnp.where(s < count, sc, -1e30)
            score.append(sc)
            dprob.append(out[:, D:])
            high = jnp.max(sc, axis=0, keepdims=True)
            top = high if top is None else jnp.maximum(top, high)
        total = 0.0
        for s in range(slots):
            score[s] = jnp.exp2(score[s] - top)
            total = total + jnp.sum(score[s], axis=0, keepdims=True)
        inverse = 1.0 / total
        delta = 0.0
        low = []
        for s in range(slots):
            score[s] = score[s] * inverse
            low.append(score[s].astype(jnp.bfloat16))
            delta = delta + jnp.sum(low[s].astype(jnp.float32) * dprob[s], axis=0, keepdims=True)
        dlow = []
        for s in range(slots):
            dlow.append((score[s] * (dprob[s] - delta)).astype(jnp.bfloat16))
            terms = jnp.dot(
                jnp.concatenate([dlow[s], low[s]], 1), both, preferred_element_type=jnp.float32
            )
            acc[idx[s]] += terms
        dq = jnp.dot(
            jnp.concatenate([kt[idx[s]] for s in range(slots)], 1), jnp.concatenate(dlow, 0),
            preferred_element_type=jnp.float32,
        )
        dq_ref[r] = (dq * scale).T.astype(jnp.bfloat16)
        return carry

    lax.fori_loop(0, nblk, block, 0)

    def finish(j, carry):
        own_ref[j, :, 0:D] = acc[j, :, 0:D] * scale
        own_ref[j, :, D : 2 * D] = acc[j, :, D : 2 * D]
        near_ref[j, :, 0:D] = (acc[nblk + j, :, 0:D] * scale).astype(jnp.bfloat16)
        near_ref[j, :, D : 2 * D] = acc[nblk + j, :, D : 2 * D].astype(jnp.bfloat16)
        return carry

    lax.fori_loop(0, nblk, finish, 0)


def attend(lists, counts, q, g, kv):
    nblk, nkey = q.shape[0], kv.shape[0]
    bf16, f32 = jnp.bfloat16, jnp.float32
    return pl.pallas_call(
        attend_kernel,
        out_shape=(
            jax.ShapeDtypeStruct((nblk, D, D), bf16),
            jax.ShapeDtypeStruct((nblk, D, 2 * D), f32),
            jax.ShapeDtypeStruct((2 * NEAR, D, 2 * D), bf16),
        ),
        in_specs=[SMEM, SMEM, VMEM, VMEM, VMEM],
        out_specs=(VMEM, VMEM, VMEM),
        scratch_shapes=[pltpu.VMEM((nkey, D, D), bf16), pltpu.VMEM((nkey, D, 2 * D), f32)],
        compiler_params=pltpu.CompilerParams(vmem_limit_bytes=56 * 2**20),
        name="attend",
    )(lists, counts, q, g, kv)


def scatter_kernel(tiles, frames, named_ref, rank_ref, dq_ref, own_ref, part_ref, dq_out, dk_out, dv_out,
                   own, parts, total, send_sem, recv_sem, local_sem, near_send, near_recv):
    me, frame = lax.axis_index("tile"), lax.axis_index("frame")
    before, after = (frame + frames - 1) % frames, (frame + 1) % frames
    greet(tiles, me, before, after)
    mine = pl.ds(pl.multiple_of(me * D, D), D)

    load = pltpu.make_async_copy(own_ref, own, local_sem.at[3])
    load.start()
    near = []
    for side, frame_to in ((0, before), (1, after)):
        copy = pltpu.make_async_remote_copy(
            src_ref=part_ref.at[pl.ds(side * NEAR, NEAR)], dst_ref=parts.at[1 - side],
            send_sem=near_send.at[side], recv_sem=near_recv.at[side],
            device_id={"frame": frame_to}, device_id_type=MESH,
        )
        copy.start()
        near.append(copy)

    def send_dq(i, carry):
        to = peer_of(i, me, tiles)
        pltpu.make_async_remote_copy(
            src_ref=dq_ref.at[to], dst_ref=dq_out.at[:, mine],
            send_sem=send_sem.at[0], recv_sem=recv_sem.at[0],
            device_id={"tile": to}, device_id_type=MESH,
        ).start()
        return carry

    lax.fori_loop(1, tiles, send_dq, 0)
    local = [pltpu.make_async_copy(dq_ref.at[me], dq_out.at[:, mine], local_sem.at[0])]
    local[0].start()
    load.wait()
    for copy in near:
        copy.wait()

    def add(to):
        value = own[to]
        for side in range(2):
            at = side * tiles + to
            part = parts[side, rank_ref[at]].astype(jnp.float32)
            value = value + jnp.where(named_ref[at] > 0, part, 0.0)
        total[to] = value.astype(jnp.bfloat16)

    def send(i, carry):
        to = peer_of(i, me, tiles)
        add(to)
        for a, out in ((1, dk_out), (2, dv_out)):
            pltpu.make_async_remote_copy(
                src_ref=total.at[to, :, pl.ds((a - 1) * D, D)], dst_ref=out.at[:, mine],
                send_sem=send_sem.at[a], recv_sem=recv_sem.at[a],
                device_id={"tile": to}, device_id_type=MESH,
            ).start()
        return carry

    lax.fori_loop(1, tiles, send, 0)
    add(me)
    for a, out in ((1, dk_out), (2, dv_out)):
        copy = pltpu.make_async_copy(total.at[me, :, pl.ds((a - 1) * D, D)], out.at[:, mine], local_sem.at[a])
        copy.start()
        local.append(copy)
    for copy in local:
        copy.wait()
    for a in range(3):
        wait_bytes(dq_out.at[:, pl.ds(0, (tiles - 1) * D)], recv_sem.at[a])
        wait_bytes(dq_out.at[:, pl.ds(0, (tiles - 1) * D)], send_sem.at[a])


def scatter(tiles, frames, named, rank, dq, own, part):
    bf16 = jnp.bfloat16
    out = jax.ShapeDtypeStruct((D, tiles * D), bf16)
    return pl.pallas_call(
        functools.partial(scatter_kernel, tiles, frames),
        out_shape=(out, out, out),
        in_specs=[SMEM, SMEM, ANY, ANY, ANY],
        out_specs=(ANY, ANY, ANY),
        scratch_shapes=[
            pltpu.VMEM((tiles, D, 2 * D), jnp.float32),
            pltpu.VMEM((2, NEAR, D, 2 * D), bf16),
            pltpu.VMEM((tiles, D, 2 * D), bf16),
            pltpu.SemaphoreType.DMA((3,)),
            pltpu.SemaphoreType.DMA((3,)),
            pltpu.SemaphoreType.DMA((4,)),
            pltpu.SemaphoreType.DMA((2,)),
            pltpu.SemaphoreType.DMA((2,)),
        ],
        compiler_params=pltpu.CompilerParams(
            collective_id=1, has_side_effects=True, vmem_limit_bytes=32 * 2**20
        ),
        name="scatter",
    )(named, rank, dq, own, part)


def naming(lists, start, nblk):
    ids = jnp.arange(nblk, dtype=jnp.int32)
    named = jnp.any(lists.reshape(-1)[:, None] == ids[None, :] + start, axis=0)
    rank = jnp.sum(jnp.where((ids[:, None] < ids[None, :]) & named[:, None], 1, 0), axis=0).astype(jnp.int32)
    return named.astype(jnp.int32), jnp.minimum(rank, NEAR - 1)


def picks(named, rank):
    ids = jnp.arange(named.shape[0], dtype=jnp.int32)
    slot = jnp.arange(NEAR, dtype=jnp.int32)
    hit = (named[None, :] > 0) & (rank[None, :] == slot[:, None])
    return jnp.sum(jnp.where(hit, ids[None, :], 0), axis=1).astype(jnp.int32)


def compact(lists, nblk):
    (_, before), (_, after) = naming(lists, 0, nblk), naming(lists, 2 * nblk, nblk)
    place = jnp.concatenate([nblk + before, jnp.arange(nblk, dtype=jnp.int32), nblk + NEAR + after])
    hit = lists[:, :, None] == jnp.arange(3 * nblk, dtype=jnp.int32)
    return jnp.sum(jnp.where(hit, place, 0), axis=2).astype(jnp.int32)


def local(tiles, frames, queries, keys, values, out_grad, key_lists, key_counts):
    nblk = key_lists.shape[0]
    of_before = lax.ppermute(key_lists, "frame", [(i, (i + 1) % frames) for i in range(frames)])
    of_after = lax.ppermute(key_lists, "frame", [(i, (i - 1) % frames) for i in range(frames)])
    named_before, rank_before = naming(of_before, 2 * nblk, nblk)
    named_after, rank_after = naming(of_after, 0, nblk)
    pick = jnp.concatenate([picks(named_before, rank_before), picks(named_after, rank_after)])
    named = jnp.concatenate([named_before, named_after])
    rank = jnp.concatenate([rank_before, rank_after])

    q, g, kv = gather(tiles, frames, pick, queries, keys, values, out_grad)
    dq, own, part = attend(compact(key_lists, nblk), key_counts, q, g, kv)
    return scatter(tiles, frames, named, rank, dq, own, part)


def solution(mesh):
    both = P(("frame", "tile"), None)
    return jax.shard_map(
        functools.partial(local, mesh.shape["tile"], mesh.shape["frame"]),
        mesh=mesh,
        in_specs=(both, both, both, both, P("frame", None), P("frame")),
        out_specs=(both, both, both),
        check_vma=False,
    )
```

```python
import functools

import jax
import jax.numpy as jnp
from jax import lax
from jax.experimental import pallas as pl
from jax.experimental.pallas import tpu as pltpu
from jax.sharding import PartitionSpec as P

D = 128
NEAR = 16
MESH = pl.DeviceIdType.MESH
ANY = pl.BlockSpec(memory_space=pl.ANY)
VMEM = pl.BlockSpec(memory_space=pltpu.VMEM)
SCALE = D ** (-0.5)
LOG2E = 1.4426950408889634
GROUP = 4
STEPS = 8
PLACE, PAIR, QUERY, SAME, LAST, HAS, COUNT, NAMED, RANK, PICK = 0, 1, 2, 3, 4, 5, 6, 7, 9, 11


def peer_of(i, me, tiles):
    half = tiles // 2
    z, y, x = me // half, (me % half) // 4, me % 4
    z = (z + i) % 2
    x = (x + i // 2) % 4
    y = (y + i // 8) % (half // 4)
    return z * half + y * 4 + x


def greet(tiles, me, before, after):
    barrier = pltpu.get_barrier_semaphore()

    def hello(i, carry):
        pl.semaphore_signal(barrier, inc=1, device_id={"tile": peer_of(i, me, tiles)}, device_id_type=MESH)
        return carry

    lax.fori_loop(1, tiles, hello, 0)
    for frame in (before, after):
        pl.semaphore_signal(barrier, inc=1, device_id={"frame": frame}, device_id_type=MESH)
    pl.semaphore_wait(barrier, tiles + 1)


def wait_bytes(ref, sem):
    pltpu.make_async_copy(ref, ref, sem).wait()


def iota(shape, axis):
    return lax.broadcasted_iota(jnp.int32, shape, axis)


def add_up(x, axis):
    return jnp.sum(x, axis=axis, keepdims=True)


def down(row):
    return jnp.broadcast_to(row, (128, 128)).T


def naming(lists, slots, nblk):
    w = iota((nblk, 128), 1)
    hits = [(lists[:, s : s + 1] == w).astype(jnp.int32) for s in range(slots)]
    named = functools.reduce(jnp.maximum, hits)
    named = jnp.max(named, axis=0, keepdims=True)
    a, b = iota((128, 128), 0), iota((128, 128), 1)

    def group(x):
        return (x >= nblk).astype(jnp.int32) + (x >= 2 * nblk).astype(jnp.int32)

    rank = add_up(jnp.where((a < b) & (group(a) == group(b)), down(named), 0), 0)
    return hits, named, jnp.minimum(rank, NEAR - 1)


def own_table(lists, slots, nblk, table):
    hits, _, rank = naming(lists, slots, nblk)
    w = iota((1, 128), 1)
    place = jnp.where(w < nblk, nblk + rank, jnp.where(w < 2 * nblk, w - nblk, nblk + NEAR + rank))
    pairs = nblk * slots
    at = jnp.concatenate([add_up(hit * place, 1) for hit in hits], 0)
    at = jnp.broadcast_to(at, (pairs, 256))
    p, t = iota((pairs, 256), 0), iota((pairs, 256), 1)
    key = at * 256 + p
    padded = jnp.concatenate([key[:, :128], jnp.full((256 - pairs, 128), 1 << 20, jnp.int32)], 0)
    row = jnp.concatenate([padded[:128].T[0:1], padded[128:].T[0:1]], 1)
    order = add_up((row < key).astype(jnp.int32), 1)
    here, ahead = order == t, order + 1 == t
    sorted_place = add_up(jnp.where(here, at, 0), 0)
    place_before = add_up(jnp.where(ahead, at, 0), 0)
    first = iota((1, 256), 1) == 0
    r = iota((nblk, 256), 0)
    rows = {
        PLACE: add_up(jnp.where(p == t, at, 0), 0),
        PAIR: add_up(jnp.where(here, p, 0), 0),
        QUERY: add_up(jnp.where(here, p % nblk, 0), 0),
        SAME: jnp.where(first, 0, (sorted_place == place_before).astype(jnp.int32)),
        LAST: jnp.maximum(add_up((at <= t).astype(jnp.int32), 0) - 1, 0),
        HAS: add_up((at == t).astype(jnp.int32), 0),
        COUNT: add_up(jnp.where(r == iota((nblk, 256), 1), lists[:, slots : slots + 1], 0), 0),
    }
    for i, value in rows.items():
        table[i : i + 1, :] = value


def near_table(lists, slots, nblk, start, side, table):
    _, named, rank = naming(lists, slots, nblk)
    w, n = iota((128, 128), 0), iota((128, 128), 1)
    hit = (down(named) > 0) & (down(rank) == n) & (w >= start) & (w < start + nblk)
    table[NAMED + side : NAMED + side + 1, 0:128] = named
    table[RANK + side : RANK + side + 1, 0:128] = rank
    table[PICK + side : PICK + side + 1, 0:128] = add_up(jnp.where(hit, w - start, 0), 0)


def f32dot(a, b):
    return jnp.dot(a, b, preferred_element_type=jnp.float32)


def attend(rs, counts, places, slots, nblk, q_ref, g_ref, kv_ref, kt_ref, terms_ref, dq_ref):
    both, score, dprob, top, low = [], [], [], [], []
    for r in rs:
        q, g = q_ref[r], g_ref[r]
        zero = jnp.zeros_like(q)
        both.append(jnp.concatenate([jnp.concatenate([q, zero], 1), jnp.concatenate([zero, g], 1)], 0))
    for b, count, place in zip(both, counts, places):
        score.append([])
        dprob.append([])
        high = None
        for s in range(slots):
            out = lax.dot_general(
                kv_ref[place[s]], b, (((1,), (1,)), ((), ())), preferred_element_type=jnp.float32
            )
            x = out[:, :D] * (SCALE * LOG2E)
            if s >= 2:
                x = jnp.where(s < count, x, -1e30)
            score[-1].append(x)
            dprob[-1].append(out[:, D:])
            x = jnp.max(x, axis=0, keepdims=True)
            high = x if high is None else jnp.maximum(high, x)
        top.append(high)
    inverse = []
    for x, high in zip(score, top):
        total = 0.0
        for s in range(slots):
            x[s] = jnp.exp2(x[s] - high)
            total = total + jnp.sum(x[s], axis=0, keepdims=True)
        inverse.append(1.0 / total)
    for a, r in enumerate(rs):
        delta = 0.0
        for s in range(slots):
            score[a][s] = score[a][s] * inverse[a]
            low = score[a][s].astype(jnp.bfloat16)
            terms_ref[s * nblk + r, :, D : 2 * D] = low
            delta = delta + jnp.sum(low.astype(jnp.float32) * dprob[a][s], axis=0, keepdims=True)
        dlow = []
        for s in range(slots):
            dlow.append((score[a][s] * (dprob[a][s] - delta)).astype(jnp.bfloat16))
            terms_ref[s * nblk + r, :, 0:D] = dlow[s]
        dq = f32dot(
            jnp.concatenate([kt_ref[places[a][s]] for s in range(slots)], 1), jnp.concatenate(dlow, 0)
        )
        dq_ref[r] = (dq * SCALE).T.astype(jnp.bfloat16)


def kernel(tiles, frames, slots, lists_ref, q_in, k_in, v_in, g_in, dq_out, dk_out, dv_out,
           own, kv, packed, parts, q_ref, g_ref, kt, terms, sums, dq_ref, near_lists, table, scalars,
           send_sem, recv_sem, local_sem, near_send, near_recv):
    nblk = tiles
    pairs = nblk * slots
    me, frame = lax.axis_index("tile"), lax.axis_index("frame")
    before, after = (frame + frames - 1) % frames, (frame + 1) % frames
    mine = pl.ds(pl.multiple_of(me * D, D), D)
    greet(tiles, me, before, after)

    def to_neighbours(stage, sources, targets):
        copies = []
        for side, frame_to in ((0, before), (1, after)):
            copies.append(pltpu.make_async_remote_copy(
                src_ref=sources[side], dst_ref=targets[1 - side],
                send_sem=near_send.at[stage, side], recv_sem=near_recv.at[stage, side],
                device_id={"frame": frame_to}, device_id_type=MESH,
            ))
        return copies

    list_copies = to_neighbours(0, [lists_ref, lists_ref], [near_lists.at[0], near_lists.at[1]])
    for copy in list_copies:
        copy.start()
    lands = (
        lambda t: own.at[t, :, pl.ds(0, D)],
        lambda t: own.at[t, :, pl.ds(D, D)],
        lambda t: q_ref.at[t],
        lambda t: g_ref.at[t],
    )
    local = []
    for a, src in enumerate((k_in, v_in, q_in, g_in)):
        def send(i, carry, a=a, src=src):
            to = peer_of(i, me, tiles)
            pltpu.make_async_remote_copy(
                src_ref=src.at[:, pl.ds(pl.multiple_of(to * D, D), D)], dst_ref=lands[a](me),
                send_sem=send_sem.at[a], recv_sem=recv_sem.at[a],
                device_id={"tile": to}, device_id_type=MESH,
            ).start()
            return carry

        lax.fori_loop(1, tiles, send, 0)
        local.append(pltpu.make_async_copy(src.at[:, mine], lands[a](me), local_sem.at[a]))
        local[a].start()

    table[...] = jnp.zeros_like(table)
    own_table(lists_ref[...], slots, nblk, table)
    for copy in list_copies:
        copy.wait()
    near_table(near_lists[0], slots, nblk, 2 * nblk, 0, table)
    near_table(near_lists[1], slots, nblk, 0, 1, table)
    to_scalars = pltpu.make_async_copy(table, scalars, local_sem.at[4])
    to_scalars.start()
    to_scalars.wait()

    for a in range(2):
        wait_bytes(own.at[pl.ds(0, tiles - 1), :, pl.ds(0, D)], recv_sem.at[a])
        local[a].wait()
    for side in range(2):
        def pack(n, carry, side=side):
            packed[side, n] = own[scalars[PICK + side, n]]
            return carry

        lax.fori_loop(0, NEAR, pack, 0)
    kv_copies = to_neighbours(
        1, [packed.at[0], packed.at[1]], [kv.at[pl.ds(nblk, NEAR)], kv.at[pl.ds(nblk + NEAR, NEAR)]]
    )
    for copy in kv_copies:
        copy.start()
    keep = pltpu.make_async_copy(own, kv.at[pl.ds(0, nblk)], local_sem.at[4])
    keep.start()

    def turn_own(j, carry):
        kt[j] = own[j, :, 0:D].T
        return carry

    lax.fori_loop(0, nblk, turn_own, 0)
    for a in range(2, 4):
        wait_bytes(q_ref.at[pl.ds(0, tiles - 1)], recv_sem.at[a])
        local[a].wait()
    keep.wait()
    for copy in kv_copies:
        copy.wait()

    def turn_near(j, carry):
        kt[nblk + j] = kv[nblk + j, :, 0:D].T
        return carry

    lax.fori_loop(0, 2 * NEAR, turn_near, 0)

    def blocks(i, carry):
        rs = [peer_of(i * GROUP + a, me, tiles) for a in range(GROUP)]
        attend(
            rs, [scalars[COUNT, r] for r in rs],
            [[scalars[PLACE, s * nblk + r] for s in range(slots)] for r in rs],
            slots, nblk, q_ref, g_ref, kv, kt, terms, dq_ref,
        )
        for a, r in enumerate(rs):
            @pl.when(i * GROUP + a > 0)
            def _(r=r):
                pltpu.make_async_remote_copy(
                    src_ref=dq_ref.at[r], dst_ref=dq_out.at[:, mine],
                    send_sem=send_sem.at[4], recv_sem=recv_sem.at[4],
                    device_id={"tile": r}, device_id_type=MESH,
                ).start()
        return carry

    lax.fori_loop(0, nblk // GROUP, blocks, 0)
    finals = [pltpu.make_async_copy(dq_ref.at[me], dq_out.at[:, mine], local_sem.at[5])]
    finals[0].start()

    def add(i, total):
        for u in range(STEPS):
            t = i * STEPS + u
            term = terms[scalars[PAIR, t]]
            r = scalars[QUERY, t]
            term = jnp.concatenate([f32dot(term[:, :D], q_ref[r]), f32dot(term[:, D:], g_ref[r])], 1)
            total = jnp.where(scalars[SAME, t] > 0, total, 0.0) + term
            sums[t] = total
        return total

    lax.fori_loop(0, pairs // STEPS, add, jnp.zeros((D, 2 * D), jnp.float32))

    def summed(j):
        total = jnp.where(scalars[HAS, j] > 0, sums[scalars[LAST, j]], 0.0)
        return jnp.concatenate([total[:, :D] * SCALE, total[:, D:]], 1)

    for side in range(2):
        def part(n, carry, side=side):
            packed[side, n] = summed(nblk + side * NEAR + n).astype(jnp.bfloat16)
            return carry

        lax.fori_loop(0, NEAR, part, 0)
    part_copies = to_neighbours(2, [packed.at[0], packed.at[1]], [parts.at[0], parts.at[1]])
    for copy in part_copies:
        copy.start()
    for copy in part_copies:
        copy.wait()

    def settle(to):
        total = summed(to)
        for side, start in ((0, 2 * nblk), (1, 0)):
            named, rank = scalars[NAMED + side, start + to], scalars[RANK + side, start + to]
            total = total + jnp.where(named > 0, parts[side, rank].astype(jnp.float32), 0.0)
        own[to] = total.astype(jnp.bfloat16)

    def send_back(i, carry):
        to = peer_of(i, me, tiles)
        settle(to)
        for a, out in ((0, dk_out), (1, dv_out)):
            pltpu.make_async_remote_copy(
                src_ref=own.at[to, :, pl.ds(a * D, D)], dst_ref=out.at[:, mine],
                send_sem=send_sem.at[5 + a], recv_sem=recv_sem.at[5 + a],
                device_id={"tile": to}, device_id_type=MESH,
            ).start()
        return carry

    lax.fori_loop(1, tiles, send_back, 0)
    settle(me)
    for a, out in ((0, dk_out), (1, dv_out)):
        copy = pltpu.make_async_copy(own.at[me, :, pl.ds(a * D, D)], out.at[:, mine], local_sem.at[6 + a])
        copy.start()
        finals.append(copy)
    for copy in finals:
        copy.wait()
    for a in range(7):
        wait_bytes(q_ref.at[pl.ds(0, tiles - 1)], send_sem.at[a])
    for a in range(4, 7):
        wait_bytes(q_ref.at[pl.ds(0, tiles - 1)], recv_sem.at[a])


def local(tiles, frames, queries, keys, values, out_grad, key_lists, key_counts):
    nblk, slots = key_lists.shape
    bf16, f32, i32 = jnp.bfloat16, jnp.float32, jnp.int32
    lists = jnp.concatenate([key_lists, key_counts[:, None]], 1)
    lists = jnp.pad(lists, ((0, 0), (0, 128 - slots - 1)), constant_values=-1)
    out = jax.ShapeDtypeStruct((D, tiles * D), bf16)
    return pl.pallas_call(
        functools.partial(kernel, tiles, frames, slots),
        out_shape=(out, out, out),
        in_specs=[VMEM, ANY, ANY, ANY, ANY],
        out_specs=(ANY, ANY, ANY),
        scratch_shapes=[
            pltpu.VMEM((nblk, D, 2 * D), bf16),
            pltpu.VMEM((nblk + 2 * NEAR, D, 2 * D), bf16),
            pltpu.VMEM((2, NEAR, D, 2 * D), bf16),
            pltpu.VMEM((2, NEAR, D, 2 * D), bf16),
            pltpu.VMEM((nblk, D, D), bf16),
            pltpu.VMEM((nblk, D, D), bf16),
            pltpu.VMEM((nblk + 2 * NEAR, D, D), bf16),
            pltpu.VMEM((nblk * slots, D, 2 * D), bf16),
            pltpu.VMEM((nblk * slots, D, 2 * D), f32),
            pltpu.VMEM((nblk, D, D), bf16),
            pltpu.VMEM((2, nblk, 128), i32),
            pltpu.VMEM((16, 256), i32),
            pltpu.SMEM((16, 256), i32),
            pltpu.SemaphoreType.DMA((7,)),
            pltpu.SemaphoreType.DMA((7,)),
            pltpu.SemaphoreType.DMA((8,)),
            pltpu.SemaphoreType.DMA((3, 2)),
            pltpu.SemaphoreType.DMA((3, 2)),
        ],
        compiler_params=pltpu.CompilerParams(
            collective_id=0, has_side_effects=True, vmem_limit_bytes=60 * 2**20
        ),
        name="backward",
    )(lists, queries, keys, values, out_grad)


def solution(mesh):
    both = P(("frame", "tile"), None)
    return jax.shard_map(
        functools.partial(local, mesh.shape["tile"], mesh.shape["frame"]),
        mesh=mesh,
        in_specs=(both, both, both, both, P("frame", None), P("frame")),
        out_specs=(both, both, both),
        check_vma=False,
    )
```

```python
import functools

import jax
import jax.numpy as jnp
from jax import lax
from jax.experimental import pallas as pl
from jax.experimental.pallas import tpu as pltpu
from jax.sharding import PartitionSpec as P

D = 128
NEAR = 16
MESH = pl.DeviceIdType.MESH
ANY = pl.BlockSpec(memory_space=pl.ANY)
VMEM = pl.BlockSpec(memory_space=pltpu.VMEM)
SCALE = D ** (-0.5)
LOG2E = 1.4426950408889634
GROUP = 4
STEPS = 8
PLACE, PAIR, QUERY, SAME, LAST, HAS, COUNT, NAMED, RANK, PICK = 0, 1, 2, 3, 4, 5, 6, 7, 9, 11


def peer_of(i, me, tiles):
    half = tiles // 2
    z, y, x = lax.div(me, half), lax.div(lax.rem(me, half), 4), lax.rem(me, 4)
    z = lax.rem(z + i, 2)
    x = lax.rem(x + lax.div(i, 2), 4)
    y = lax.rem(y + lax.div(i, 8), half // 4)
    return z * half + y * 4 + x


def sender_of(i, me, tiles):
    half = tiles // 2
    z, y, x = lax.div(me, half), lax.div(lax.rem(me, half), 4), lax.rem(me, 4)
    z = lax.rem(z + i, 2)
    x = lax.rem(x + 4 - lax.rem(lax.div(i, 2), 4), 4)
    y = lax.rem(y + half // 4 - lax.div(i, 8), half // 4)
    return z * half + y * 4 + x


def near_first(k, tiles):
    return lax.rem(2 * k, tiles) + lax.div(k, tiles // 2)


def far_first(k, tiles):
    return 2 * k - 1 - lax.div(k, tiles // 2 + 1) * (tiles - 1)


def greet(tiles, me, before, after):
    barrier = pltpu.get_barrier_semaphore()

    def hello(i, carry):
        pl.semaphore_signal(barrier, inc=1, device_id={"tile": peer_of(i, me, tiles)}, device_id_type=MESH)
        return carry

    lax.fori_loop(1, tiles, hello, 0)
    for frame in (before, after):
        pl.semaphore_signal(barrier, inc=1, device_id={"frame": frame}, device_id_type=MESH)
    pl.semaphore_wait(barrier, tiles + 1)


def wait_bytes(ref, sem):
    pltpu.make_async_copy(ref, ref, sem).wait()


def iota(shape, axis):
    return lax.broadcasted_iota(jnp.int32, shape, axis)


def add_up(x, axis):
    return jnp.sum(x, axis=axis, keepdims=True)


def down(row):
    return jnp.broadcast_to(row, (128, 128)).T


def turned(lists, nblk):
    rest = jnp.zeros((128 - lists.shape[0], 128), jnp.int32)
    return jnp.concatenate([lists, rest], 0).T[:nblk]


def naming(lists, slots, nblk):
    w = iota((nblk, 128), 1)
    hits = [(lists[:, s : s + 1] == w).astype(jnp.int32) for s in range(slots)]
    named = functools.reduce(jnp.maximum, hits)
    named = jnp.max(named, axis=0, keepdims=True)
    a, b = iota((128, 128), 0), iota((128, 128), 1)

    def group(x):
        return (x >= nblk).astype(jnp.int32) + (x >= 2 * nblk).astype(jnp.int32)

    rank = add_up(jnp.where((a < b) & (group(a) == group(b)), down(named), 0), 0)
    return hits, named, jnp.minimum(rank, NEAR - 1)


def own_table(lists, slots, nblk, table):
    hits, _, rank = naming(lists, slots, nblk)
    w = iota((1, 128), 1)
    place = jnp.where(w < nblk, nblk + rank, jnp.where(w < 2 * nblk, w - nblk, nblk + NEAR + rank))
    pairs = nblk * slots
    at = jnp.concatenate([add_up(hit * place, 1) for hit in hits], 0)
    at = jnp.broadcast_to(at, (pairs, 256))
    p, t = iota((pairs, 256), 0), iota((pairs, 256), 1)
    key = at * 256 + p
    padded = jnp.concatenate([key[:, :128], jnp.full((256 - pairs, 128), 1 << 20, jnp.int32)], 0)
    row = jnp.concatenate([padded[:128].T[0:1], padded[128:].T[0:1]], 1)
    order = add_up((row < key).astype(jnp.int32), 1)
    here, ahead = order == t, order + 1 == t
    sorted_place = add_up(jnp.where(here, at, 0), 0)
    place_before = add_up(jnp.where(ahead, at, 0), 0)
    first = iota((1, 256), 1) == 0
    rows = {
        PLACE: add_up(jnp.where(p == t, at, 0), 0),
        PAIR: add_up(jnp.where(here, p, 0), 0),
        QUERY: add_up(jnp.where(here, p % nblk, 0), 0),
        SAME: jnp.where(first, 0, (sorted_place == place_before).astype(jnp.int32)),
        LAST: jnp.maximum(add_up((at <= t).astype(jnp.int32), 0) - 1, 0),
        HAS: add_up((at == t).astype(jnp.int32), 0),
    }
    for i, value in rows.items():
        table[i : i + 1, :] = value


def near_table(lists, slots, nblk, start, side, table):
    _, named, rank = naming(lists, slots, nblk)
    w, n = iota((128, 128), 0), iota((128, 128), 1)
    hit = (down(named) > 0) & (down(rank) == n) & (w >= start) & (w < start + nblk)
    table[NAMED + side : NAMED + side + 1, 0:128] = named
    table[RANK + side : RANK + side + 1, 0:128] = rank
    table[PICK + side : PICK + side + 1, 0:128] = add_up(jnp.where(hit, w - start, 0), 0)


def f32dot(a, b):
    return jnp.dot(a, b, preferred_element_type=jnp.float32)


def attend(rs, counts, places, slots, nblk, q_ref, g_ref, kv_ref, kt_ref, terms_ref, dq_ref):
    both, score, dprob, top, low = [], [], [], [], []
    for r in rs:
        q, g = q_ref[r], g_ref[r]
        zero = jnp.zeros_like(q)
        both.append(jnp.concatenate([jnp.concatenate([q, zero], 1), jnp.concatenate([zero, g], 1)], 0))
    for b, count, place in zip(both, counts, places):
        score.append([])
        dprob.append([])
        high = None
        for s in range(slots):
            out = lax.dot_general(
                kv_ref[place[s]], b, (((1,), (1,)), ((), ())), preferred_element_type=jnp.float32
            )
            x = out[:, :D] * (SCALE * LOG2E)
            if s >= 2:
                x = jnp.where(s < count, x, -1e30)
            score[-1].append(x)
            dprob[-1].append(out[:, D:])
            x = jnp.max(x, axis=0, keepdims=True)
            high = x if high is None else jnp.maximum(high, x)
        top.append(high)
    inverse = []
    for x, high in zip(score, top):
        total = 0.0
        for s in range(slots):
            x[s] = jnp.exp2(x[s] - high)
            total = total + jnp.sum(x[s], axis=0, keepdims=True)
        inverse.append(1.0 / total)
    for a, r in enumerate(rs):
        delta = 0.0
        for s in range(slots):
            score[a][s] = score[a][s] * inverse[a]
            low = score[a][s].astype(jnp.bfloat16)
            terms_ref[s * nblk + r, :, D : 2 * D] = low
            delta = delta + jnp.sum(low.astype(jnp.float32) * dprob[a][s], axis=0, keepdims=True)
        dlow = []
        for s in range(slots):
            dlow.append((score[a][s] * (dprob[a][s] - delta)).astype(jnp.bfloat16))
            terms_ref[s * nblk + r, :, 0:D] = dlow[s]
        dq = f32dot(
            jnp.concatenate([kt_ref[places[a][s]] for s in range(slots)], 1), jnp.concatenate(dlow, 0)
        )
        dq_ref[r] = (dq * SCALE).T.astype(jnp.bfloat16)


def kernel(tiles, frames, slots, lists_in, counts_in, q_in, k_in, v_in, g_in, dq_out, dk_out, dv_out,
           own_k, own_v, kv, packed, parts_k, parts_v, q_ref, g_ref, kt, terms, sums, dq_ref, own_lists, counts, lists_ref, near_lists, table, scalars,
           send_sem, recv_sem, qg_sem, local_sem, near_send, near_recv):
    nblk = tiles
    pairs = nblk * slots
    me, frame = lax.axis_index("tile"), lax.axis_index("frame")
    before, after = lax.rem(frame + frames - 1, frames), lax.rem(frame + 1, frames)
    mine = pl.ds(pl.multiple_of(me * D, D), D)
    loads = [
        pltpu.make_async_copy(lists_in, own_lists, local_sem.at[4]),
        pltpu.make_async_copy(counts_in, counts, local_sem.at[5]),
    ]
    for copy in loads:
        copy.start()
    greet(tiles, me, before, after)

    def to_neighbours(stage, sources, targets):
        copies = []
        for side, frame_to in ((0, before), (1, after)):
            copies.append(pltpu.make_async_remote_copy(
                src_ref=sources[side], dst_ref=targets[1 - side],
                send_sem=near_send.at[stage, side], recv_sem=near_recv.at[stage, side],
                device_id={"frame": frame_to}, device_id_type=MESH,
            ))
        return copies

    def gather(src, place, start, stop, sent, arrived):
        def send(i, carry):
            to = peer_of(i, me, tiles)
            pltpu.make_async_remote_copy(
                src_ref=src.at[:, pl.ds(pl.multiple_of(to * D, D), D)], dst_ref=place(me),
                send_sem=sent, recv_sem=arrived(i),
                device_id={"tile": to}, device_id_type=MESH,
            ).start()
            return carry

        lax.fori_loop(start, stop, send, 0)

    def keep_own(src, place, sem):
        copy = pltpu.make_async_copy(src.at[:, mine], place(me), sem)
        copy.start()
        return copy

    own = (own_k, own_v)
    kv_land = (lambda t: own_k.at[t], lambda t: own_v.at[t])
    qg_land = (lambda t: q_ref.at[t], lambda t: g_ref.at[t])
    local = []
    for a, src in enumerate((k_in, v_in)):
        gather(src, kv_land[a], 1, tiles, send_sem.at[a], lambda i: recv_sem.at[a])
        local.append(keep_own(src, kv_land[a], local_sem.at[a]))

    def gather_qg(start, stop):
        def send(i, carry):
            i = near_first(i, tiles)
            to = peer_of(i, me, tiles)
            for a, src in enumerate((q_in, g_in)):
                pltpu.make_async_remote_copy(
                    src_ref=src.at[:, pl.ds(pl.multiple_of(to * D, D), D)], dst_ref=qg_land[a](me),
                    send_sem=send_sem.at[2 + a], recv_sem=qg_sem.at[a, i],
                    device_id={"tile": to}, device_id_type=MESH,
                ).start()
            return carry

        lax.fori_loop(start, stop, send, 0)

    for a, src in enumerate((q_in, g_in)):
        local.append(keep_own(src, qg_land[a], qg_sem.at[a, 0]))
    gather_qg(1, tiles // 2)

    for copy in loads:
        copy.wait()
    lists_ref[...] = jnp.zeros_like(lists_ref)
    lists_ref[0:slots, 0:nblk] = own_lists[...]
    list_copies = to_neighbours(0, [lists_ref, lists_ref], [near_lists.at[0], near_lists.at[1]])
    for copy in list_copies:
        copy.start()

    table[...] = jnp.zeros_like(table)
    table[COUNT : COUNT + 1, 0:nblk] = counts[...]
    own_table(turned(lists_ref[...], nblk), slots, nblk, table)
    for copy in list_copies:
        copy.wait()
    near_table(turned(near_lists[0], nblk), slots, nblk, 2 * nblk, 0, table)
    near_table(turned(near_lists[1], nblk), slots, nblk, 0, 1, table)
    to_scalars = pltpu.make_async_copy(table, scalars, local_sem.at[4])
    to_scalars.start()
    to_scalars.wait()

    keep, kv_copies = [], []
    for a in range(2):
        wait_bytes(own[a].at[pl.ds(0, tiles - 1)], recv_sem.at[a])
        local[a].wait()
        for side in range(2):
            def pack(n, carry, a=a, side=side):
                packed[a, side, n] = own[a][scalars[PICK + side, n]]
                return carry

            lax.fori_loop(0, NEAR, pack, 0)
        cut = pl.ds(a * D, D)
        kv_copies += to_neighbours(
            1 + a, [packed.at[a, 0], packed.at[a, 1]],
            [kv.at[pl.ds(nblk, NEAR), :, cut], kv.at[pl.ds(nblk + NEAR, NEAR), :, cut]],
        )
        for copy in kv_copies[-2:]:
            copy.start()
        keep.append(pltpu.make_async_copy(own[a], kv.at[pl.ds(0, nblk), :, cut], local_sem.at[4 + a]))
        keep[a].start()
    gather_qg(tiles // 2, tiles)

    def turn_own(j, carry):
        kt[j] = own_k[j].T
        return carry

    lax.fori_loop(0, nblk, turn_own, 0)
    for copy in keep + kv_copies:
        copy.wait()

    def turn_near(j, carry):
        kt[nblk + j] = kv[nblk + j, :, 0:D].T
        return carry

    lax.fori_loop(0, 2 * NEAR, turn_near, 0)

    def blocks(i, carry):
        steps = [near_first(i * GROUP + a, tiles) for a in range(GROUP)]
        rs = [sender_of(step, me, tiles) for step in steps]
        for a, r in enumerate(rs):
            for b, place in enumerate(qg_land):
                wait_bytes(place(r), qg_sem.at[b, steps[a]])
        attend(
            rs, [scalars[COUNT, r] for r in rs],
            [[scalars[PLACE, s * nblk + r] for s in range(slots)] for r in rs],
            slots, nblk, q_ref, g_ref, kv, kt, terms, dq_ref,
        )
        return carry

    lax.fori_loop(0, nblk // GROUP, blocks, 0)

    def send_dq(i, carry):
        to = peer_of(far_first(i, tiles), me, tiles)
        pltpu.make_async_remote_copy(
            src_ref=dq_ref.at[to], dst_ref=dq_out.at[:, mine],
            send_sem=send_sem.at[4], recv_sem=recv_sem.at[4],
            device_id={"tile": to}, device_id_type=MESH,
        ).start()
        return carry

    lax.fori_loop(1, tiles, send_dq, 0)
    finals = [pltpu.make_async_copy(dq_ref.at[me], dq_out.at[:, mine], local_sem.at[0])]
    finals[0].start()

    def add(i, total):
        for u in range(STEPS):
            t = i * STEPS + u
            term = terms[scalars[PAIR, t]]
            r = scalars[QUERY, t]
            term = jnp.concatenate([f32dot(term[:, :D], q_ref[r]), f32dot(term[:, D:], g_ref[r])], 1)
            total = jnp.where(scalars[SAME, t] > 0, total, 0.0) + term
            sums[t] = total
        return total

    lax.fori_loop(0, pairs // STEPS, add, jnp.zeros((D, 2 * D), jnp.float32))

    parts = (parts_k, parts_v)
    part_copies = []
    for a in (1, 0):
        cut = pl.ds(a * D, D)
        for side in range(2):
            def part(n, carry, a=a, side=side, cut=cut):
                j = nblk + side * NEAR + n
                total = jnp.where(scalars[HAS, j] > 0, sums[scalars[LAST, j], :, cut], 0.0)
                if a == 0:
                    total = total * SCALE
                packed[a, side, n] = total.astype(jnp.bfloat16)
                return carry

            lax.fori_loop(0, NEAR, part, 0)
        part_copies.append(to_neighbours(
            3 + a, [packed.at[a, side] for side in range(2)], [parts[a].at[side] for side in range(2)]
        ))
        for copy in part_copies[-1]:
            copy.start()

    for a, out, copies in ((1, dv_out, part_copies[0]), (0, dk_out, part_copies[1])):
        cut = pl.ds(a * D, D)
        for copy in copies:
            copy.wait()

        def settle(to, cut=cut, a=a):
            total = jnp.where(scalars[HAS, to] > 0, sums[scalars[LAST, to], :, cut], 0.0)
            if a == 0:
                total = total * SCALE
            for side, start in ((0, 2 * nblk), (1, 0)):
                named, rank = scalars[NAMED + side, start + to], scalars[RANK + side, start + to]
                total = total + jnp.where(named > 0, parts[a][side, rank].astype(jnp.float32), 0.0)
            own[a][to] = total.astype(jnp.bfloat16)

        def send_back(i, carry, a=a, out=out, settle=settle):
            to = peer_of((far_first, near_first)[a](i, tiles), me, tiles)
            settle(to)
            pltpu.make_async_remote_copy(
                src_ref=own[a].at[to], dst_ref=out.at[:, mine],
                send_sem=send_sem.at[5 + a], recv_sem=recv_sem.at[5 + a],
                device_id={"tile": to}, device_id_type=MESH,
            ).start()
            return carry

        lax.fori_loop(1, tiles, send_back, 0)
        settle(me)
        copy = pltpu.make_async_copy(own[a].at[me], out.at[:, mine], local_sem.at[1 + a])
        copy.start()
        finals.append(copy)
    for copy in finals:
        copy.wait()
    for a in range(7):
        wait_bytes(q_ref.at[pl.ds(0, tiles - 1)], send_sem.at[a])
    for a in range(4, 7):
        wait_bytes(q_ref.at[pl.ds(0, tiles - 1)], recv_sem.at[a])


def hand_over(a_in, b_in, c_in, a_out, b_out, c_out, sem):
    copies = []
    for i, (src, dst) in enumerate(((a_in, a_out), (b_in, b_out), (c_in, c_out))):
        copies.append(pltpu.make_async_copy(src, dst, sem.at[i]))
        copies[-1].start()
    for copy in copies:
        copy.wait()


def local(tiles, frames, queries, keys, values, out_grad, key_lists, key_counts):
    nblk, slots = key_lists.shape
    bf16, f32, i32 = jnp.bfloat16, jnp.float32, jnp.int32
    out = jax.ShapeDtypeStruct((D, tiles * D), bf16)
    grads = pl.pallas_call(
        functools.partial(kernel, tiles, frames, slots),
        out_shape=(out, out, out),
        in_specs=[ANY] * 6,
        out_specs=(ANY, ANY, ANY),
        scratch_shapes=[
            pltpu.VMEM((nblk, D, D), bf16),
            pltpu.VMEM((nblk, D, D), bf16),
            pltpu.VMEM((nblk + 2 * NEAR, D, 2 * D), bf16),
            pltpu.VMEM((2, 2, NEAR, D, D), bf16),
            pltpu.VMEM((2, NEAR, D, D), bf16),
            pltpu.VMEM((2, NEAR, D, D), bf16),
            pltpu.VMEM((nblk, D, D), bf16),
            pltpu.VMEM((nblk, D, D), bf16),
            pltpu.VMEM((nblk + 2 * NEAR, D, D), bf16),
            pltpu.VMEM((nblk * slots, D, 2 * D), bf16),
            pltpu.VMEM((nblk * slots, D, 2 * D), f32),
            pltpu.VMEM((nblk, D, D), bf16),
            pltpu.VMEM((slots, nblk), i32),
            pltpu.VMEM((1, nblk), i32),
            pltpu.VMEM((8, 128), i32),
            pltpu.VMEM((2, 8, 128), i32),
            pltpu.VMEM((16, 256), i32),
            pltpu.SMEM((16, 256), i32),
            pltpu.SemaphoreType.DMA((7,)),
            pltpu.SemaphoreType.DMA((7,)),
            pltpu.SemaphoreType.DMA((2, nblk)),
            pltpu.SemaphoreType.DMA((6,)),
            pltpu.SemaphoreType.DMA((5, 2)),
            pltpu.SemaphoreType.DMA((5, 2)),
        ],
        compiler_params=pltpu.CompilerParams(
            collective_id=0, has_side_effects=True, vmem_limit_bytes=60 * 2**20
        ),
        name="backward",
    )(key_lists.T, key_counts[None, :], queries, keys, values, out_grad)
    return pl.pallas_call(
        hand_over,
        out_shape=(out, out, out),
        in_specs=[VMEM] * 3,
        out_specs=(ANY, ANY, ANY),
        scratch_shapes=[pltpu.SemaphoreType.DMA((3,))],
        name="hand_over",
    )(*grads)


def solution(mesh):
    both = P(("frame", "tile"), None)
    return jax.shard_map(
        functools.partial(local, mesh.shape["tile"], mesh.shape["frame"]),
        mesh=mesh,
        in_specs=(both, both, both, both, P("frame", None), P("frame")),
        out_specs=(both, both, both),
        check_vma=False,
    )
```

```python
import functools

import jax
import jax.numpy as jnp
from jax import lax
from jax.experimental import pallas as pl
from jax.experimental.pallas import tpu as pltpu
from jax.sharding import PartitionSpec as P

D = 128
NEAR = 16
MESH = pl.DeviceIdType.MESH
ANY = pl.BlockSpec(memory_space=pl.ANY)
SCALE = D ** (-0.5)
LOG2E = 1.4426950408889634
GROUP = 4
STEPS = 16
PLACE, PAIR, QUERY, SAME, LAST, HAS, COUNT, NAMED, RANK, PICK = 0, 1, 2, 3, 4, 5, 6, 7, 9, 11


def peer_of(i, me, tiles):
    half = tiles // 2
    z, y, x = lax.div(me, half), lax.div(lax.rem(me, half), 4), lax.rem(me, 4)
    z = lax.rem(z + i, 2)
    x = lax.rem(x + lax.div(i, 2), 4)
    y = lax.rem(y + lax.div(i, 8), half // 4)
    return z * half + y * 4 + x


def sender_of(i, me, tiles):
    half = tiles // 2
    z, y, x = lax.div(me, half), lax.div(lax.rem(me, half), 4), lax.rem(me, 4)
    z = lax.rem(z + i, 2)
    x = lax.rem(x + 4 - lax.rem(lax.div(i, 2), 4), 4)
    y = lax.rem(y + half // 4 - lax.div(i, 8), half // 4)
    return z * half + y * 4 + x


def near_first(k, tiles):
    return lax.rem(2 * k, tiles) + lax.div(k, tiles // 2)


def far_first(k, tiles):
    return 2 * k - 1 - lax.div(k, tiles // 2 + 1) * (tiles - 1)


def greet(tiles, me, before, after):
    barrier = pltpu.get_barrier_semaphore()

    def hello(i, carry):
        pl.semaphore_signal(barrier, inc=1, device_id={"tile": peer_of(i, me, tiles)}, device_id_type=MESH)
        return carry

    lax.fori_loop(1, tiles, hello, 0)
    for frame in (before, after):
        pl.semaphore_signal(barrier, inc=1, device_id={"frame": frame}, device_id_type=MESH)
    pl.semaphore_wait(barrier, tiles + 1)


def wait_bytes(ref, sem):
    pltpu.make_async_copy(ref, ref, sem).wait()


def iota(shape, axis):
    return lax.broadcasted_iota(jnp.int32, shape, axis)


def add_up(x, axis):
    return jnp.sum(x, axis=axis, keepdims=True)


def down(row):
    return jnp.broadcast_to(row, (128, 128)).T


def turned(lists, nblk):
    rest = jnp.zeros((128 - lists.shape[0], 128), jnp.int32)
    return jnp.concatenate([lists, rest], 0).T[:nblk]


def naming(lists, slots, nblk):
    w = iota((nblk, 128), 1)
    hits = [(lists[:, s : s + 1] == w).astype(jnp.int32) for s in range(slots)]
    named = functools.reduce(jnp.maximum, hits)
    named = jnp.max(named, axis=0, keepdims=True)
    a, b = iota((128, 128), 0), iota((128, 128), 1)

    def group(x):
        return (x >= nblk).astype(jnp.int32) + (x >= 2 * nblk).astype(jnp.int32)

    rank = add_up(jnp.where((a < b) & (group(a) == group(b)), down(named), 0), 0)
    return hits, named, jnp.minimum(rank, NEAR - 1)


def own_table(lists, slots, nblk, table):
    hits, _, rank = naming(lists, slots, nblk)
    w = iota((1, 128), 1)
    place = jnp.where(w < nblk, nblk + rank, jnp.where(w < 2 * nblk, w - nblk, nblk + NEAR + rank))
    pairs = nblk * slots
    at = jnp.concatenate([add_up(hit * place, 1) for hit in hits], 0)
    at = jnp.broadcast_to(at, (pairs, 256))
    p, t = iota((pairs, 256), 0), iota((pairs, 256), 1)
    key = at * 256 + p
    padded = jnp.concatenate([key[:, :128], jnp.full((256 - pairs, 128), 1 << 20, jnp.int32)], 0)
    row = jnp.concatenate([padded[:128].T[0:1], padded[128:].T[0:1]], 1)
    order = add_up((row < key).astype(jnp.int32), 1)
    here, ahead = order == t, order + 1 == t
    sorted_place = add_up(jnp.where(here, at, 0), 0)
    place_before = add_up(jnp.where(ahead, at, 0), 0)
    first = iota((1, 256), 1) == 0
    rows = {
        PLACE: add_up(jnp.where(p == t, at, 0), 0),
        PAIR: add_up(jnp.where(here, p, 0), 0),
        QUERY: add_up(jnp.where(here, p % nblk, 0), 0),
        SAME: jnp.where(first, 0, (sorted_place == place_before).astype(jnp.int32)),
        LAST: jnp.maximum(add_up((at <= t).astype(jnp.int32), 0) - 1, 0),
        HAS: add_up((at == t).astype(jnp.int32), 0),
    }
    for i, value in rows.items():
        table[i : i + 1, :] = value


def near_table(lists, slots, nblk, start, side, table):
    _, named, rank = naming(lists, slots, nblk)
    w, n = iota((128, 128), 0), iota((128, 128), 1)
    hit = (down(named) > 0) & (down(rank) == n) & (w >= start) & (w < start + nblk)
    table[NAMED + side : NAMED + side + 1, 0:128] = named
    table[RANK + side : RANK + side + 1, 0:128] = rank
    table[PICK + side : PICK + side + 1, 0:128] = add_up(jnp.where(hit, w - start, 0), 0)


def f32dot(a, b):
    return jnp.dot(a, b, preferred_element_type=jnp.float32)


def attend(rs, counts, places, slots, nblk, q_ref, g_ref, kv_ref, kt_ref, terms_ref, dq_ref):
    both, score, dprob, top, low = [], [], [], [], []
    for r in rs:
        q, g = q_ref[r], g_ref[r]
        zero = jnp.zeros_like(q)
        both.append(jnp.concatenate([jnp.concatenate([q, zero], 1), jnp.concatenate([zero, g], 1)], 0))
    for b, count, place in zip(both, counts, places):
        score.append([])
        dprob.append([])
        high = None
        for s in range(slots):
            out = lax.dot_general(
                kv_ref[place[s]], b, (((1,), (1,)), ((), ())), preferred_element_type=jnp.float32
            )
            x = out[:, :D] * (SCALE * LOG2E)
            if s >= 2:
                x = jnp.where(s < count, x, -1e30)
            score[-1].append(x)
            dprob[-1].append(out[:, D:])
            x = jnp.max(x, axis=0, keepdims=True)
            high = x if high is None else jnp.maximum(high, x)
        top.append(high)
    inverse = []
    for x, high in zip(score, top):
        total = 0.0
        for s in range(slots):
            x[s] = jnp.exp2(x[s] - high)
            total = total + jnp.sum(x[s], axis=0, keepdims=True)
        inverse.append(1.0 / total)
    for a, r in enumerate(rs):
        delta = 0.0
        for s in range(slots):
            score[a][s] = score[a][s] * inverse[a]
            low = score[a][s].astype(jnp.bfloat16)
            terms_ref[s * nblk + r, :, D : 2 * D] = low
            delta = delta + jnp.sum(low.astype(jnp.float32) * dprob[a][s], axis=0, keepdims=True)
        dlow = []
        for s in range(slots):
            dlow.append((score[a][s] * (dprob[a][s] - delta)).astype(jnp.bfloat16))
            terms_ref[s * nblk + r, :, 0:D] = dlow[s]
        dq = f32dot(
            jnp.concatenate([kt_ref[places[a][s]] for s in range(slots)], 1), jnp.concatenate(dlow, 0)
        )
        dq_ref[r] = (dq * SCALE).T.astype(jnp.bfloat16)


def kernel(tiles, frames, slots, lists_in, counts_in, q_in, k_in, v_in, g_in, dq_out, dk_out, dv_out,
           own_k, own_v, kv, packed, parts_k, parts_v, q_ref, g_ref, kt, terms, sums, dq_ref, own_lists, counts, lists_ref, near_lists, table, scalars, staged,
           send_sem, recv_sem, qg_sem, stage_sem, local_sem, near_send, near_recv):
    nblk = tiles
    pairs = nblk * slots
    me, frame = lax.axis_index("tile"), lax.axis_index("frame")
    before, after = lax.rem(frame + frames - 1, frames), lax.rem(frame + 1, frames)
    mine = pl.ds(pl.multiple_of(me * D, D), D)
    loads = [
        pltpu.make_async_copy(lists_in, own_lists, local_sem.at[4]),
        pltpu.make_async_copy(counts_in, counts, local_sem.at[5]),
    ]
    for copy in loads:
        copy.start()
    stage = []
    for a, src in enumerate((k_in, v_in, q_in, g_in)):
        stage.append(pltpu.make_async_copy(src, staged.at[a], stage_sem.at[a]))
        stage[a].start()
    greet(tiles, me, before, after)

    def to_neighbours(stage, sources, targets):
        copies = []
        for side, frame_to in ((0, before), (1, after)):
            copies.append(pltpu.make_async_remote_copy(
                src_ref=sources[side], dst_ref=targets[1 - side],
                send_sem=near_send.at[stage, side], recv_sem=near_recv.at[stage, side],
                device_id={"frame": frame_to}, device_id_type=MESH,
            ))
        return copies

    for copy in loads:
        copy.wait()
    lists_ref[...] = jnp.zeros_like(lists_ref)
    lists_ref[0:slots, 0:nblk] = own_lists[...]
    list_copies = to_neighbours(0, [lists_ref, lists_ref], [near_lists.at[0], near_lists.at[1]])
    for copy in list_copies:
        copy.start()


    def gather(src, place, start, stop, sent, arrived):
        def send(i, carry):
            to = peer_of(i, me, tiles)
            pltpu.make_async_remote_copy(
                src_ref=src.at[:, pl.ds(pl.multiple_of(to * D, D), D)], dst_ref=place(me),
                send_sem=sent, recv_sem=arrived(i),
                device_id={"tile": to}, device_id_type=MESH,
            ).start()
            return carry

        lax.fori_loop(start, stop, send, 0)

    def keep_own(src, place, sem):
        copy = pltpu.make_async_copy(src.at[:, mine], place(me), sem)
        copy.start()
        return copy

    own = (own_k, own_v)
    kv_land = (lambda t: own_k.at[t], lambda t: own_v.at[t])
    qg_land = (lambda t: q_ref.at[t], lambda t: g_ref.at[t])
    local = []
    for a, src in enumerate((k_in, v_in)):
        stage[a].wait()
        gather(staged.at[a], kv_land[a], 1, tiles, send_sem.at[a], lambda i: recv_sem.at[a])
        local.append(keep_own(src, kv_land[a], local_sem.at[a]))

    def gather_qg(start, stop):
        def send(i, carry):
            i = near_first(i, tiles)
            to = peer_of(i, me, tiles)
            for a in range(2):
                pltpu.make_async_remote_copy(
                    src_ref=staged.at[2 + a, :, pl.ds(pl.multiple_of(to * D, D), D)], dst_ref=qg_land[a](me),
                    send_sem=send_sem.at[2 + a], recv_sem=qg_sem.at[a, i],
                    device_id={"tile": to}, device_id_type=MESH,
                ).start()
            return carry

        lax.fori_loop(start, stop, send, 0)

    for a, src in enumerate((q_in, g_in)):
        local.append(keep_own(src, qg_land[a], qg_sem.at[a, 0]))
    stage[2].wait()
    stage[3].wait()

    table[...] = jnp.zeros_like(table)
    table[COUNT : COUNT + 1, 0:nblk] = counts[...]
    own_table(turned(lists_ref[...], nblk), slots, nblk, table)
    for copy in list_copies:
        copy.wait()
    near_table(turned(near_lists[0], nblk), slots, nblk, 2 * nblk, 0, table)
    near_table(turned(near_lists[1], nblk), slots, nblk, 0, 1, table)
    to_scalars = pltpu.make_async_copy(table, scalars, local_sem.at[4])
    to_scalars.start()
    to_scalars.wait()

    keep, kv_copies = [], []
    for a in range(2):
        wait_bytes(own[a].at[pl.ds(0, tiles - 1)], recv_sem.at[a])
        local[a].wait()
        for side in range(2):
            def pack(n, carry, a=a, side=side):
                packed[a, side, n] = own[a][scalars[PICK + side, n]]
                return carry

            lax.fori_loop(0, NEAR, pack, 0)
        cut = pl.ds(a * D, D)
        kv_copies += to_neighbours(
            1 + a, [packed.at[a, 0], packed.at[a, 1]],
            [kv.at[pl.ds(nblk, NEAR), :, cut], kv.at[pl.ds(nblk + NEAR, NEAR), :, cut]],
        )
        for copy in kv_copies[-2:]:
            copy.start()
        if a == 0:
            gather_qg(1, tiles // 2)
        keep.append(pltpu.make_async_copy(own[a], kv.at[pl.ds(0, nblk), :, cut], local_sem.at[4 + a]))
        keep[a].start()
    gather_qg(tiles // 2, tiles)

    def turn_own(j, carry):
        kt[j] = own_k[j].T
        return carry

    lax.fori_loop(0, nblk, turn_own, 0)
    for copy in keep + kv_copies:
        copy.wait()

    def turn_near(j, carry):
        kt[nblk + j] = kv[nblk + j, :, 0:D].T
        return carry

    lax.fori_loop(0, 2 * NEAR, turn_near, 0)

    def blocks(i, carry):
        steps = [near_first(i * GROUP + a, tiles) for a in range(GROUP)]
        rs = [sender_of(step, me, tiles) for step in steps]
        for a, r in enumerate(rs):
            for b, place in enumerate(qg_land):
                wait_bytes(place(r), qg_sem.at[b, steps[a]])
        attend(
            rs, [scalars[COUNT, r] for r in rs],
            [[scalars[PLACE, s * nblk + r] for s in range(slots)] for r in rs],
            slots, nblk, q_ref, g_ref, kv, kt, terms, dq_ref,
        )
        for step, r in zip(steps, rs):
            @pl.when(step > 0)
            def _(r=r):
                pltpu.make_async_remote_copy(
                    src_ref=dq_ref.at[r], dst_ref=dq_out.at[:, mine],
                    send_sem=send_sem.at[4], recv_sem=recv_sem.at[4],
                    device_id={"tile": r}, device_id_type=MESH,
                ).start()
        return carry

    lax.fori_loop(0, nblk // GROUP, blocks, 0)
    finals = [pltpu.make_async_copy(dq_ref.at[me], dq_out.at[:, mine], local_sem.at[0])]
    finals[0].start()

    parts = (parts_k, parts_v)
    part_copies = []
    for a, rows in ((1, g_ref), (0, q_ref)):
        cut = pl.ds(a * D, D)

        def add(i, total, rows=rows, cut=cut):
            for u in range(STEPS):
                t = i * STEPS + u
                term = f32dot(terms[scalars[PAIR, t], :, cut], rows[scalars[QUERY, t]])
                total = jnp.where(scalars[SAME, t] > 0, total, 0.0) + term
                sums[t, :, cut] = total
            return total

        lax.fori_loop(0, pairs // STEPS, add, jnp.zeros((D, D), jnp.float32))
        for side in range(2):
            def part(n, carry, a=a, side=side, cut=cut):
                j = nblk + side * NEAR + n
                total = jnp.where(scalars[HAS, j] > 0, sums[scalars[LAST, j], :, cut], 0.0)
                if a == 0:
                    total = total * SCALE
                packed[a, side, n] = total.astype(jnp.bfloat16)
                return carry

            lax.fori_loop(0, NEAR, part, 0)
        part_copies.append(to_neighbours(
            3 + a, [packed.at[a, side] for side in range(2)], [parts[a].at[side] for side in range(2)]
        ))
        for copy in part_copies[-1]:
            copy.start()

    for a, out, copies in ((1, dv_out, part_copies[0]), (0, dk_out, part_copies[1])):
        cut = pl.ds(a * D, D)
        for copy in copies:
            copy.wait()

        def settle(to, cut=cut, a=a):
            total = jnp.where(scalars[HAS, to] > 0, sums[scalars[LAST, to], :, cut], 0.0)
            if a == 0:
                total = total * SCALE
            for side, start in ((0, 2 * nblk), (1, 0)):
                named, rank = scalars[NAMED + side, start + to], scalars[RANK + side, start + to]
                total = total + jnp.where(named > 0, parts[a][side, rank].astype(jnp.float32), 0.0)
            own[a][to] = total.astype(jnp.bfloat16)

        def send_back(i, carry, a=a, out=out, settle=settle):
            to = peer_of((far_first, near_first)[a](i, tiles), me, tiles)
            settle(to)
            pltpu.make_async_remote_copy(
                src_ref=own[a].at[to], dst_ref=out.at[:, mine],
                send_sem=send_sem.at[5 + a], recv_sem=recv_sem.at[5 + a],
                device_id={"tile": to}, device_id_type=MESH,
            ).start()
            return carry

        lax.fori_loop(1, tiles, send_back, 0)
        settle(me)
        copy = pltpu.make_async_copy(own[a].at[me], out.at[:, mine], local_sem.at[1 + a])
        copy.start()
        finals.append(copy)
    for copy in finals:
        copy.wait()
    for a in range(7):
        wait_bytes(q_ref.at[pl.ds(0, tiles - 1)], send_sem.at[a])
    for a in range(4, 7):
        wait_bytes(q_ref.at[pl.ds(0, tiles - 1)], recv_sem.at[a])


def hand_over(a_in, b_in, c_in, a_out, b_out, c_out, held, in_sem, out_sem):
    loads, stores = [], []
    for i, (src, dst) in enumerate(((a_in, a_out), (b_in, b_out), (c_in, c_out))):
        for j in range(2):
            rows = pl.ds(j * (D // 2), D // 2)
            loads.append(pltpu.make_async_copy(src.at[rows], held.at[i, rows], in_sem.at[i, j]))
            stores.append(pltpu.make_async_copy(held.at[i, rows], dst.at[rows], out_sem.at[i, j]))
            loads[-1].start()
    for load, store in zip(loads, stores):
        load.wait()
        store.start()
    for store in stores:
        store.wait()


def local(tiles, frames, queries, keys, values, out_grad, key_lists, key_counts):
    nblk, slots = key_lists.shape
    bf16, f32, i32 = jnp.bfloat16, jnp.float32, jnp.int32
    out = jax.ShapeDtypeStruct((D, tiles * D), bf16)
    grads = pl.pallas_call(
        functools.partial(kernel, tiles, frames, slots),
        out_shape=(out, out, out),
        in_specs=[ANY] * 6,
        out_specs=(ANY, ANY, ANY),
        scratch_shapes=[
            pltpu.VMEM((nblk, D, D), bf16),
            pltpu.VMEM((nblk, D, D), bf16),
            pltpu.VMEM((nblk + 2 * NEAR, D, 2 * D), bf16),
            pltpu.VMEM((2, 2, NEAR, D, D), bf16),
            pltpu.VMEM((2, NEAR, D, D), bf16),
            pltpu.VMEM((2, NEAR, D, D), bf16),
            pltpu.VMEM((nblk, D, D), bf16),
            pltpu.VMEM((nblk, D, D), bf16),
            pltpu.VMEM((nblk + 2 * NEAR, D, D), bf16),
            pltpu.VMEM((nblk * slots, D, 2 * D), bf16),
            pltpu.VMEM((nblk * slots, D, 2 * D), f32),
            pltpu.VMEM((nblk, D, D), bf16),
            pltpu.VMEM((slots, nblk), i32),
            pltpu.VMEM((1, nblk), i32),
            pltpu.VMEM((8, 128), i32),
            pltpu.VMEM((2, 8, 128), i32),
            pltpu.VMEM((16, 256), i32),
            pltpu.SMEM((16, 256), i32),
            pltpu.VMEM((4, D, tiles * D), bf16),
            pltpu.SemaphoreType.DMA((7,)),
            pltpu.SemaphoreType.DMA((7,)),
            pltpu.SemaphoreType.DMA((2, nblk)),
            pltpu.SemaphoreType.DMA((4,)),
            pltpu.SemaphoreType.DMA((6,)),
            pltpu.SemaphoreType.DMA((5, 2)),
            pltpu.SemaphoreType.DMA((5, 2)),
        ],
        compiler_params=pltpu.CompilerParams(
            collective_id=0, has_side_effects=True, vmem_limit_bytes=60 * 2**20
        ),
        name="backward",
    )(key_lists.T, key_counts[None, :], queries, keys, values, out_grad)
    return pl.pallas_call(
        hand_over,
        out_shape=(out, out, out),
        in_specs=[ANY] * 3,
        out_specs=(ANY, ANY, ANY),
        scratch_shapes=[
            pltpu.VMEM((3, D, tiles * D), bf16),
            pltpu.SemaphoreType.DMA((3, 2)),
            pltpu.SemaphoreType.DMA((3, 2)),
        ],
        compiler_params=pltpu.CompilerParams(vmem_limit_bytes=60 * 2**20),
        name="hand_over",
    )(*grads)


def solution(mesh):
    both = P(("frame", "tile"), None)
    return jax.shard_map(
        functools.partial(local, mesh.shape["tile"], mesh.shape["frame"]),
        mesh=mesh,
        in_specs=(both, both, both, both, P("frame", None), P("frame")),
        out_specs=(both, both, both),
        check_vma=False,
    )
```

```python
import functools

import jax
import jax.numpy as jnp
from jax import lax
from jax.experimental import pallas as pl
from jax.experimental.pallas import tpu as pltpu
from jax.sharding import PartitionSpec as P

D = 128
NEAR = 16
MESH = pl.DeviceIdType.MESH
ANY = pl.BlockSpec(memory_space=pl.ANY)
SCALE = D ** (-0.5)
LOG2E = 1.4426950408889634
GROUP = 4
STEPS = 32
PLACE, PAIR, QUERY, SAME, LAST, HAS, COUNT, NAMED, RANK, PICK = 0, 1, 2, 3, 4, 5, 6, 7, 9, 11


def peer_of(i, me, tiles):
    half = tiles // 2
    z, y, x = lax.div(me, half), lax.div(lax.rem(me, half), 4), lax.rem(me, 4)
    z = lax.rem(z + i, 2)
    x = lax.rem(x + lax.div(i, 2), 4)
    y = lax.rem(y + lax.div(i, 8), half // 4)
    return z * half + y * 4 + x


def sender_of(i, me, tiles):
    half = tiles // 2
    z, y, x = lax.div(me, half), lax.div(lax.rem(me, half), 4), lax.rem(me, 4)
    z = lax.rem(z + i, 2)
    x = lax.rem(x + 4 - lax.rem(lax.div(i, 2), 4), 4)
    y = lax.rem(y + half // 4 - lax.div(i, 8), half // 4)
    return z * half + y * 4 + x


def near_first(k, tiles):
    return lax.rem(2 * k, tiles) + lax.div(k, tiles // 2)


def far_first(k, tiles):
    return 2 * k - 1 - lax.div(k, tiles // 2 + 1) * (tiles - 1)


def greet(tiles, me, before, after):
    barrier = pltpu.get_barrier_semaphore()

    def hello(i, carry):
        pl.semaphore_signal(barrier, inc=1, device_id={"tile": peer_of(i, me, tiles)}, device_id_type=MESH)
        return carry

    lax.fori_loop(1, tiles, hello, 0)
    for frame in (before, after):
        pl.semaphore_signal(barrier, inc=1, device_id={"frame": frame}, device_id_type=MESH)
    pl.semaphore_wait(barrier, tiles + 1)


def wait_bytes(ref, sem):
    pltpu.make_async_copy(ref, ref, sem).wait()


def iota(shape, axis):
    return lax.broadcasted_iota(jnp.int32, shape, axis)


def add_up(x, axis):
    return jnp.sum(x, axis=axis, keepdims=True)


def down(row):
    return jnp.broadcast_to(row, (128, 128)).T


def turned(lists, nblk):
    rest = jnp.zeros((128 - lists.shape[0], 128), jnp.int32)
    return jnp.concatenate([lists, rest], 0).T[:nblk]


def naming(lists, slots, nblk):
    w = iota((nblk, 128), 1)
    hits = [(lists[:, s : s + 1] == w).astype(jnp.int32) for s in range(slots)]
    named = functools.reduce(jnp.maximum, hits)
    named = jnp.max(named, axis=0, keepdims=True)
    a, b = iota((128, 128), 0), iota((128, 128), 1)

    def group(x):
        return (x >= nblk).astype(jnp.int32) + (x >= 2 * nblk).astype(jnp.int32)

    rank = add_up(jnp.where((a < b) & (group(a) == group(b)), down(named), 0), 0)
    return hits, named, jnp.minimum(rank, NEAR - 1)


def own_table(lists, slots, nblk, table):
    hits, _, rank = naming(lists, slots, nblk)
    w = iota((1, 128), 1)
    place = jnp.where(w < nblk, nblk + rank, jnp.where(w < 2 * nblk, w - nblk, nblk + NEAR + rank))
    pairs = nblk * slots
    at = jnp.concatenate([add_up(hit * place, 1) for hit in hits], 0)
    at = jnp.broadcast_to(at, (pairs, 256))
    p, t = iota((pairs, 256), 0), iota((pairs, 256), 1)
    key = at * 256 + p
    padded = jnp.concatenate([key[:, :128], jnp.full((256 - pairs, 128), 1 << 20, jnp.int32)], 0)
    row = jnp.concatenate([padded[:128].T[0:1], padded[128:].T[0:1]], 1)
    order = add_up((row < key).astype(jnp.int32), 1)
    here, ahead = order == t, order + 1 == t
    sorted_place = add_up(jnp.where(here, at, 0), 0)
    place_before = add_up(jnp.where(ahead, at, 0), 0)
    first = iota((1, 256), 1) == 0
    rows = {
        PLACE: add_up(jnp.where(p == t, at, 0), 0),
        PAIR: add_up(jnp.where(here, p, 0), 0),
        QUERY: add_up(jnp.where(here, p % nblk, 0), 0),
        SAME: jnp.where(first, 0, (sorted_place == place_before).astype(jnp.int32)),
        LAST: jnp.maximum(add_up((at <= t).astype(jnp.int32), 0) - 1, 0),
        HAS: add_up((at == t).astype(jnp.int32), 0),
    }
    for i, value in rows.items():
        table[i : i + 1, :] = value


def near_table(lists, slots, nblk, start, side, table):
    _, named, rank = naming(lists, slots, nblk)
    w, n = iota((128, 128), 0), iota((128, 128), 1)
    hit = (down(named) > 0) & (down(rank) == n) & (w >= start) & (w < start + nblk)
    table[NAMED + side : NAMED + side + 1, 0:128] = named
    table[RANK + side : RANK + side + 1, 0:128] = rank
    table[PICK + side : PICK + side + 1, 0:128] = add_up(jnp.where(hit, w - start, 0), 0)


def f32dot(a, b):
    return jnp.dot(a, b, preferred_element_type=jnp.float32)


def attend(rs, counts, places, slots, nblk, q_ref, g_ref, kv_ref, kt_ref, terms_ref, dq_ref):
    both, score, dprob, top, low = [], [], [], [], []
    for r in rs:
        q, g = q_ref[r], g_ref[r]
        zero = jnp.zeros_like(q)
        both.append(jnp.concatenate([jnp.concatenate([q, zero], 1), jnp.concatenate([zero, g], 1)], 0))
    for b, count, place in zip(both, counts, places):
        score.append([])
        dprob.append([])
        high = None
        for s in range(slots):
            out = lax.dot_general(
                kv_ref[place[s]], b, (((1,), (1,)), ((), ())), preferred_element_type=jnp.float32
            )
            x = out[:, :D] * (SCALE * LOG2E)
            if s >= 2:
                x = jnp.where(s < count, x, -1e30)
            score[-1].append(x)
            dprob[-1].append(out[:, D:])
            x = jnp.max(x, axis=0, keepdims=True)
            high = x if high is None else jnp.maximum(high, x)
        top.append(high)
    inverse = []
    for x, high in zip(score, top):
        total = 0.0
        for s in range(slots):
            x[s] = jnp.exp2(x[s] - high)
            total = total + jnp.sum(x[s], axis=0, keepdims=True)
        inverse.append(1.0 / total)
    for a, r in enumerate(rs):
        delta = 0.0
        for s in range(slots):
            score[a][s] = score[a][s] * inverse[a]
            low = score[a][s].astype(jnp.bfloat16)
            terms_ref[s * nblk + r, :, D : 2 * D] = low
            delta = delta + jnp.sum(low.astype(jnp.float32) * dprob[a][s], axis=0, keepdims=True)
        dlow = []
        for s in range(slots):
            dlow.append((score[a][s] * (dprob[a][s] - delta)).astype(jnp.bfloat16))
            terms_ref[s * nblk + r, :, 0:D] = dlow[s]
        dq = f32dot(
            jnp.concatenate([kt_ref[places[a][s]] for s in range(slots)], 1), jnp.concatenate(dlow, 0)
        )
        dq_ref[r] = (dq * SCALE).T.astype(jnp.bfloat16)


def kernel(tiles, frames, slots, lists_in, counts_in, q_in, k_in, v_in, g_in, dq_out, dk_out, dv_out,
           own_k, own_v, kv, packed, parts_k, parts_v, q_ref, g_ref, kt, terms, sums, dq_ref, own_lists, counts, lists_ref, near_lists, table, scalars, staged,
           send_sem, recv_sem, qg_sem, stage_sem, local_sem, near_send, near_recv):
    nblk = tiles
    pairs = nblk * slots
    me, frame = lax.axis_index("tile"), lax.axis_index("frame")
    before, after = lax.rem(frame + frames - 1, frames), lax.rem(frame + 1, frames)
    mine = pl.ds(pl.multiple_of(me * D, D), D)
    loads = [
        pltpu.make_async_copy(lists_in, own_lists, local_sem.at[4]),
        pltpu.make_async_copy(counts_in, counts, local_sem.at[5]),
    ]
    for copy in loads:
        copy.start()
    stage = []
    for a, src in enumerate((k_in, v_in, q_in, g_in)):
        stage.append(pltpu.make_async_copy(src, staged.at[a], stage_sem.at[a]))
        stage[a].start()
    greet(tiles, me, before, after)

    def to_neighbours(stage, sources, targets):
        copies = []
        for side, frame_to in ((0, before), (1, after)):
            copies.append(pltpu.make_async_remote_copy(
                src_ref=sources[side], dst_ref=targets[1 - side],
                send_sem=near_send.at[stage, side], recv_sem=near_recv.at[stage, side],
                device_id={"frame": frame_to}, device_id_type=MESH,
            ))
        return copies

    for copy in loads:
        copy.wait()
    lists_ref[...] = jnp.zeros_like(lists_ref)
    lists_ref[0:slots, 0:nblk] = own_lists[...]
    list_copies = to_neighbours(0, [lists_ref, lists_ref], [near_lists.at[0], near_lists.at[1]])
    for copy in list_copies:
        copy.start()


    def gather(src, place, start, stop, sent, arrived):
        def send(i, carry):
            to = peer_of(i, me, tiles)
            pltpu.make_async_remote_copy(
                src_ref=src.at[:, pl.ds(pl.multiple_of(to * D, D), D)], dst_ref=place(me),
                send_sem=sent, recv_sem=arrived(i),
                device_id={"tile": to}, device_id_type=MESH,
            ).start()
            return carry

        lax.fori_loop(start, stop, send, 0)

    def keep_own(src, place, sem):
        copy = pltpu.make_async_copy(src.at[:, mine], place(me), sem)
        copy.start()
        return copy

    own = (own_k, own_v)
    kv_land = (lambda t: own_k.at[t], lambda t: own_v.at[t])
    qg_land = (lambda t: q_ref.at[t], lambda t: g_ref.at[t])
    local = []
    for a, src in enumerate((k_in, v_in)):
        stage[a].wait()
        gather(staged.at[a], kv_land[a], 1, tiles, send_sem.at[a], lambda i: recv_sem.at[a])
        local.append(keep_own(src, kv_land[a], local_sem.at[a]))

    def gather_qg(start, stop):
        def send(i, carry):
            i = near_first(i, tiles)
            to = peer_of(i, me, tiles)
            for a in range(2):
                pltpu.make_async_remote_copy(
                    src_ref=staged.at[2 + a, :, pl.ds(pl.multiple_of(to * D, D), D)], dst_ref=qg_land[a](me),
                    send_sem=send_sem.at[2 + a], recv_sem=qg_sem.at[a, i],
                    device_id={"tile": to}, device_id_type=MESH,
                ).start()
            return carry

        lax.fori_loop(start, stop, send, 0)

    for a, src in enumerate((q_in, g_in)):
        local.append(keep_own(src, qg_land[a], qg_sem.at[a, 0]))
    stage[2].wait()
    stage[3].wait()

    table[...] = jnp.zeros_like(table)
    table[COUNT : COUNT + 1, 0:nblk] = counts[...]
    own_table(turned(lists_ref[...], nblk), slots, nblk, table)
    for copy in list_copies:
        copy.wait()
    near_table(turned(near_lists[0], nblk), slots, nblk, 2 * nblk, 0, table)
    near_table(turned(near_lists[1], nblk), slots, nblk, 0, 1, table)
    to_scalars = pltpu.make_async_copy(table, scalars, local_sem.at[4])
    to_scalars.start()
    to_scalars.wait()

    keep, kv_copies = [], []
    for a in range(2):
        wait_bytes(own[a].at[pl.ds(0, tiles - 1)], recv_sem.at[a])
        local[a].wait()
        for side in range(2):
            def pack(n, carry, a=a, side=side):
                packed[a, side, n] = own[a][scalars[PICK + side, n]]
                return carry

            lax.fori_loop(0, NEAR, pack, 0)
        cut = pl.ds(a * D, D)
        kv_copies += to_neighbours(
            1 + a, [packed.at[a, 0], packed.at[a, 1]],
            [kv.at[pl.ds(nblk, NEAR), :, cut], kv.at[pl.ds(nblk + NEAR, NEAR), :, cut]],
        )
        for copy in kv_copies[-2:]:
            copy.start()
        if a == 0:
            gather_qg(1, tiles // 2)
        keep.append(pltpu.make_async_copy(own[a], kv.at[pl.ds(0, nblk), :, cut], local_sem.at[4 + a]))
        keep[a].start()
    gather_qg(tiles // 2, tiles)

    def turn_own(j, carry):
        kt[j] = own_k[j].T
        return carry

    lax.fori_loop(0, nblk, turn_own, 0)
    for copy in keep + kv_copies:
        copy.wait()

    def turn_near(j, carry):
        kt[nblk + j] = kv[nblk + j, :, 0:D].T
        return carry

    lax.fori_loop(0, 2 * NEAR, turn_near, 0)

    def blocks(i, carry):
        steps = [near_first(i * GROUP + a, tiles) for a in range(GROUP)]
        rs = [sender_of(step, me, tiles) for step in steps]
        for a, r in enumerate(rs):
            for b, place in enumerate(qg_land):
                wait_bytes(place(r), qg_sem.at[b, steps[a]])
        attend(
            rs, [scalars[COUNT, r] for r in rs],
            [[scalars[PLACE, s * nblk + r] for s in range(slots)] for r in rs],
            slots, nblk, q_ref, g_ref, kv, kt, terms, dq_ref,
        )
        for step, r in zip(steps, rs):
            @pl.when(step > 0)
            def _(r=r):
                pltpu.make_async_remote_copy(
                    src_ref=dq_ref.at[r], dst_ref=dq_out.at[:, mine],
                    send_sem=send_sem.at[4], recv_sem=recv_sem.at[4],
                    device_id={"tile": r}, device_id_type=MESH,
                ).start()
        return carry

    lax.fori_loop(0, nblk // GROUP, blocks, 0)
    finals = [pltpu.make_async_copy(dq_ref.at[me], dq_out.at[:, mine], local_sem.at[0])]
    finals[0].start()

    parts = (parts_k, parts_v)
    part_copies = []
    for a, rows in ((1, g_ref), (0, q_ref)):
        cut = pl.ds(a * D, D)

        def add(i, total, rows=rows, cut=cut):
            for u in range(STEPS):
                t = i * STEPS + u
                term = f32dot(terms[scalars[PAIR, t], :, cut], rows[scalars[QUERY, t]])
                total = jnp.where(scalars[SAME, t] > 0, total, 0.0) + term
                sums[t, :, cut] = total
            return total

        lax.fori_loop(0, pairs // STEPS, add, jnp.zeros((D, D), jnp.float32))
        for side in range(2):
            def part(n, carry, a=a, side=side, cut=cut):
                j = nblk + side * NEAR + n
                total = jnp.where(scalars[HAS, j] > 0, sums[scalars[LAST, j], :, cut], 0.0)
                if a == 0:
                    total = total * SCALE
                packed[a, side, n] = total.astype(jnp.bfloat16)
                return carry

            lax.fori_loop(0, NEAR, part, 0)
        part_copies.append(to_neighbours(
            3 + a, [packed.at[a, side] for side in range(2)], [parts[a].at[side] for side in range(2)]
        ))
        for copy in part_copies[-1]:
            copy.start()

    for a, out, copies in ((1, dv_out, part_copies[0]), (0, dk_out, part_copies[1])):
        cut = pl.ds(a * D, D)
        for copy in copies:
            copy.wait()

        def settle(to, cut=cut, a=a):
            total = jnp.where(scalars[HAS, to] > 0, sums[scalars[LAST, to], :, cut], 0.0)
            if a == 0:
                total = total * SCALE
            for side, start in ((0, 2 * nblk), (1, 0)):
                named, rank = scalars[NAMED + side, start + to], scalars[RANK + side, start + to]
                total = total + jnp.where(named > 0, parts[a][side, rank].astype(jnp.float32), 0.0)
            own[a][to] = total.astype(jnp.bfloat16)

        def send_back(i, carry, a=a, out=out, settle=settle):
            to = peer_of((far_first, near_first)[a](i, tiles), me, tiles)
            settle(to)
            pltpu.make_async_remote_copy(
                src_ref=own[a].at[to], dst_ref=out.at[:, mine],
                send_sem=send_sem.at[5 + a], recv_sem=recv_sem.at[5 + a],
                device_id={"tile": to}, device_id_type=MESH,
            ).start()
            return carry

        lax.fori_loop(1, tiles, send_back, 0)
        settle(me)
        copy = pltpu.make_async_copy(own[a].at[me], out.at[:, mine], local_sem.at[1 + a])
        copy.start()
        finals.append(copy)
    for copy in finals:
        copy.wait()
    for a in range(7):
        wait_bytes(q_ref.at[pl.ds(0, tiles - 1)], send_sem.at[a])
    for a in range(4, 7):
        wait_bytes(q_ref.at[pl.ds(0, tiles - 1)], recv_sem.at[a])


def hand_over(a_in, b_in, c_in, a_out, b_out, c_out, held, in_sem, out_sem):
    loads, stores = [], []
    for i, (src, dst) in enumerate(((a_in, a_out), (b_in, b_out), (c_in, c_out))):
        for j in range(2):
            rows = pl.ds(j * (D // 2), D // 2)
            loads.append(pltpu.make_async_copy(src.at[rows], held.at[i, rows], in_sem.at[i, j]))
            stores.append(pltpu.make_async_copy(held.at[i, rows], dst.at[rows], out_sem.at[i, j]))
            loads[-1].start()
    for load, store in zip(loads, stores):
        load.wait()
        store.start()
    for store in stores:
        store.wait()


def local(tiles, frames, queries, keys, values, out_grad, key_lists, key_counts):
    nblk, slots = key_lists.shape
    bf16, f32, i32 = jnp.bfloat16, jnp.float32, jnp.int32
    out = jax.ShapeDtypeStruct((D, tiles * D), bf16)
    grads = pl.pallas_call(
        functools.partial(kernel, tiles, frames, slots),
        out_shape=(out, out, out),
        in_specs=[ANY] * 6,
        out_specs=(ANY, ANY, ANY),
        scratch_shapes=[
            pltpu.VMEM((nblk, D, D), bf16),
            pltpu.VMEM((nblk, D, D), bf16),
            pltpu.VMEM((nblk + 2 * NEAR, D, 2 * D), bf16),
            pltpu.VMEM((2, 2, NEAR, D, D), bf16),
            pltpu.VMEM((2, NEAR, D, D), bf16),
            pltpu.VMEM((2, NEAR, D, D), bf16),
            pltpu.VMEM((nblk, D, D), bf16),
            pltpu.VMEM((nblk, D, D), bf16),
            pltpu.VMEM((nblk + 2 * NEAR, D, D), bf16),
            pltpu.VMEM((nblk * slots, D, 2 * D), bf16),
            pltpu.VMEM((nblk * slots, D, 2 * D), f32),
            pltpu.VMEM((nblk, D, D), bf16),
            pltpu.VMEM((slots, nblk), i32),
            pltpu.VMEM((1, nblk), i32),
            pltpu.VMEM((8, 128), i32),
            pltpu.VMEM((2, 8, 128), i32),
            pltpu.VMEM((16, 256), i32),
            pltpu.SMEM((16, 256), i32),
            pltpu.VMEM((4, D, tiles * D), bf16),
            pltpu.SemaphoreType.DMA((7,)),
            pltpu.SemaphoreType.DMA((7,)),
            pltpu.SemaphoreType.DMA((2, nblk)),
            pltpu.SemaphoreType.DMA((4,)),
            pltpu.SemaphoreType.DMA((6,)),
            pltpu.SemaphoreType.DMA((5, 2)),
            pltpu.SemaphoreType.DMA((5, 2)),
        ],
        compiler_params=pltpu.CompilerParams(
            collective_id=0, has_side_effects=True, vmem_limit_bytes=60 * 2**20
        ),
        name="backward",
    )(key_lists.T, key_counts[None, :], queries, keys, values, out_grad)
    return pl.pallas_call(
        hand_over,
        out_shape=(out, out, out),
        in_specs=[ANY] * 3,
        out_specs=(ANY, ANY, ANY),
        scratch_shapes=[
            pltpu.VMEM((3, D, tiles * D), bf16),
            pltpu.SemaphoreType.DMA((3, 2)),
            pltpu.SemaphoreType.DMA((3, 2)),
        ],
        compiler_params=pltpu.CompilerParams(vmem_limit_bytes=60 * 2**20),
        name="hand_over",
    )(*grads)


def solution(mesh):
    both = P(("frame", "tile"), None)
    return jax.shard_map(
        functools.partial(local, mesh.shape["tile"], mesh.shape["frame"]),
        mesh=mesh,
        in_specs=(both, both, both, both, P("frame", None), P("frame")),
        out_specs=(both, both, both),
        check_vma=False,
    )
```
